256 devices in a mesh: row: 8 (over z), col: 16 (over y, x), layer: 2 (over core).
Axes of the slice: x: 4, y: 4, z: 8, core: 2. Of those that a mesh axis runs over, the one named last changes fastest.
Arguments:
- integrals: bfloat16 [8, 4096, 4096], P('layer', 'row', 'col'), may hold values from -6 to 6
- density_occ: bfloat16 [4096, 4096], P('row', 'col'), as said below
- density_virt: bfloat16 [4096, 4096], P('row', 'col'), may hold values from -0.125 to 0.125
- mask_int: int32 [8, 32, 32], P('layer', 'row', 'col'), may hold values 0 or 1
- mask_occ: int32 [32, 32], P('row', 'col'), may hold values from 0 to 1, as said below
- mask_virt: int32 [32, 32], P('row', 'col'), may hold values 0 or 1
Outputs:
- polar_tensor: bfloat16 [8, 4096, 4096], P('layer', 'row', 'col')
- chi_block: float32 [8, 8], P('layer')
The draws below stay inside these ranges and needn't reach their ends.
Inputs may be any that keep to these rules, and one draw needn't show every extreme that they name: density_occ is symmetric. mask_occ is symmetric with ones on its diagonal.
All inputs are finite; a program needn't handle non-finite values. No bound on the sum of `mask_int` or of `mask_virt` on one device may be relied on, other than what follows from the above.
Results may differ from the reference program's by a relative error of at most 0.0054.
Values may be sent and summed in bfloat16 or wider, within the bound.
No kernel may reach another device: no remote copies, remote signals or barrier semaphores. Data moves between devices by JAX's collectives and lax.ppermute only.
A program may use at most 128 MiB of HBM per device.

```python
import jax
import jax.numpy as jnp
from jax import lax

BLK = 128
NBLK = 32
NB = 4096
NAUX = 8


def draw_density_occ(key, part):
    key = jax.random.fold_in(key, 11)
    sample = jax.random.normal(key, (NB, NB), jnp.float32)
    return ((sample + sample.T) * NB ** (-0.5)).astype(jnp.bfloat16)


def draw_mask_occ(key, part):
    key = jax.random.fold_in(key, 23)
    chosen = jax.random.randint(key, (NBLK, NBLK), 0, 3)
    marked = jnp.where(chosen == 0, 1, 0).astype(jnp.int32)
    indices = jnp.arange(NBLK, dtype=jnp.int32)
    diagonal = jnp.where(indices[:, None] == indices[None, :], 1, 0).astype(jnp.int32)
    return jnp.maximum(jnp.maximum(marked, marked.T), diagonal)


def plant(array, rng, smallest, largest):
    place = [jax.random.randint(jax.random.fold_in(rng, axis), (), 0, length) for axis, length in enumerate(array.shape)]
    longest = array.shape.index(max(array.shape))
    beside = place[:longest] + [(place[longest] + 1) % array.shape[longest]] + place[longest + 1:]
    return array.at[tuple(place)].set(smallest).at[tuple(beside)].set(largest)


def shard_levels(own_key, shape, shards, least, largest):
    gain = 1.0
    for axis_at, blocks in shards:
        heights = jax.random.uniform(jax.random.fold_in(jax.random.fold_in(own_key, 6), axis_at), (blocks,), jnp.float32, least / len(shards), largest / len(shards))
        gain = gain * jnp.repeat(jnp.exp(heights), shape[axis_at] // blocks).reshape((-1,) + (1,) * (len(shape) - 1 - axis_at))
    return gain


def bell_draw(own_key, dims, deviation, bound, shards=(), kind=jnp.bfloat16):
    entries = deviation * jax.random.normal(own_key, dims, jnp.float32)
    if shards:
        entries = entries * shard_levels(own_key, dims, shards, -0.22, 0.18)
    return jnp.clip(entries, -bound, bound).astype(kind)


def setup_inputs(seed: int = 0) -> dict:
    splits = jax.random.split(jax.random.key(seed), 7)
    return {
        "integrals": bell_draw(splits[0], (NAUX, NB, NB), 1.0, 6.0, ((0, 2), (1, 8), (2, 16))),
        "density_occ": draw_density_occ(jax.random.fold_in(splits[6], 71), 0),
        "density_virt": bell_draw(splits[2], (NB, NB), (NB // 2) ** -0.5, 0.125, ((0, 8), (1, 16))),
        "mask_int": plant((jax.random.randint(splits[3], (NAUX, NBLK, NBLK), 0, 3) < 2).astype(jnp.int32), jax.random.fold_in(splits[3], 1), 0, 1),
        "mask_occ": draw_mask_occ(jax.random.fold_in(splits[6], 71), 0),
        "mask_virt": plant((jax.random.randint(splits[5], (NBLK, NBLK), 0, 3) < 2).astype(jnp.int32), jax.random.fold_in(splits[5], 1), 0, 1),
    }


def expand_mask(blocks, block_width):
    extent = blocks.shape
    spread = jnp.broadcast_to(blocks[..., :, None, :, None], extent[:-2] + (extent[-2], block_width, extent[-1], block_width))
    return spread.reshape(extent[:-2] + (extent[-2] * block_width, extent[-1] * block_width)).astype(jnp.bfloat16)


def reference(integrals, density_occ, density_virt, mask_int, mask_occ, mask_virt):
    masked_int = integrals * expand_mask(mask_int, BLK)
    occupied = density_occ * expand_mask(mask_occ, BLK)
    virtual = density_virt * expand_mask(mask_virt, BLK)

    def one_row(aux_slice):
        half_tensor = jnp.dot(aux_slice, virtual, preferred_element_type=jnp.float32).astype(jnp.bfloat16)
        return jnp.dot(occupied, half_tensor, preferred_element_type=jnp.float32).astype(jnp.bfloat16)

    polar_tensor = lax.map(one_row, masked_int)
    flat_polar = polar_tensor.reshape(NAUX, NB * NB)
    flat_int = masked_int.reshape(NAUX, NB * NB)
    chi_block = lax.dot_general(flat_polar, flat_int, (((1,), (1,)), ((), ())), preferred_element_type=jnp.float32) * (1.0 / NB)
    return polar_tensor, chi_block
```

```python
import functools

import jax
import jax.numpy as jnp
from jax import lax
from jax.experimental import pallas as pl
from jax.experimental.pallas import tpu as pltpu
from jax.sharding import PartitionSpec as P

BLK = 128
ROWS = 512
COLS = 256
HALF = 256
PAIR = 2
F32 = jnp.float32
BF16 = jnp.bfloat16
VMEM = pl.BlockSpec(memory_space=pltpu.VMEM)
SMEM = pl.BlockSpec(memory_space=pltpu.SMEM)
PARAMS = pltpu.CompilerParams(vmem_limit_bytes=48 * 1024 * 1024)


def plane_index(y, x, core):
    return ((y % 4) * 4 + x % 4) * 2 + core


def plane_perm(shift, first):
    pairs = []
    for y in range(4):
        for x in range(4):
            for core in range(2):
                along_x = (core == 0) == first
                to = (y, x + shift) if along_x else (y + shift, x)
                pairs.append((plane_index(y, x, core), plane_index(*to, core)))
    return pairs


def plane_move(value, shift, first):
    return lax.ppermute(value, ("col", "layer"), plane_perm(shift, first))


def ring_move(value, shift):
    return lax.ppermute(value, "row", [(i, (i + shift) % 8) for i in range(8)])


def swap_cores(value):
    return lax.ppermute(value, "layer", [(0, 1), (1, 0)])


def gather_plane(value):
    before = plane_move(value, 1, True)
    after = plane_move(value, -1, True)
    across = plane_move(value, 2, True)
    near = jnp.concatenate([value, before, after, across], axis=0)
    half = near.shape[0] // 2
    second_before = plane_move(near, 1, False)
    second_after = plane_move(near, -1, False)
    top = plane_move(second_before[:half], 1, False)
    bottom = plane_move(second_after[half:], -1, False)
    return near, second_before, second_after, top, bottom


NEAR = ((0, 0), (-1, 0), (1, 0), (2, 0))
BEFORE = ((0, -1), (-1, -1), (1, -1), (2, -1))
AFTER = ((0, 1), (-1, 1), (1, 1), (2, 1))
TOP = ((0, 2), (-1, 2))
BOTTOM = ((1, 2), (2, 2))

RING = (0, -1, 1, -2, 2, -3, 3, 4, 4)


def gather_ring(value):
    half = value.shape[0] // 2
    up1, down1 = ring_move(value, 1), ring_move(value, -1)
    up2, down2 = ring_move(up1, 1), ring_move(down1, -1)
    up3, down3 = ring_move(up2, 1), ring_move(down2, -1)
    up4, down4 = ring_move(up3[:half], 1), ring_move(down3[half:], -1)
    return value, up1, down1, up2, down2, up3, down3, up4, down4


def mask_kernel(pos, mask_int, mask_occ, mask_virt, integrals, occ, virt, plane, ring, occ_half):
    def masked(ref, index, row, col, weight):
        block = ref[index + (pl.ds(row, BLK), pl.ds(col, BLK))]
        return (block.astype(F32) * weight.astype(F32)).astype(BF16)

    core = pos[3]
    for p in range(2 * PAIR):
        for i in range(ROWS // BLK):
            for j in range(COLS // BLK):
                block = masked(integrals, (p,), i * BLK, j * BLK, mask_int[p, i, j])
                cols = pl.ds(j * BLK, BLK)
                if p < PAIR:
                    plane[pl.ds(p * ROWS + i * BLK, BLK), cols] = block
                else:
                    start = (p - PAIR) * (ROWS + HALF) + i * BLK
                    ring[pl.ds(start, BLK), cols] = block
    for i in range(HALF // BLK):
        source = core * HALF + i * BLK
        source = pl.multiple_of(source, BLK)
        row = core * (HALF // BLK) + i
        for j in range(COLS // BLK):
            cols = pl.ds(j * BLK, BLK)
            ring[pl.ds(ROWS + i * BLK, BLK), cols] = masked(virt, (), source, j * BLK, mask_virt[row, j])
            occ_half[0, pl.ds(i * BLK, BLK), cols] = masked(occ, (), source, j * BLK, mask_occ[row, j])


def mask_inputs(pos, mask_int, mask_occ, mask_virt, integrals, occ, virt):
    return pl.pallas_call(
        mask_kernel,
        out_shape=(
            jax.ShapeDtypeStruct((PAIR * ROWS, COLS), BF16),
            jax.ShapeDtypeStruct((PAIR * ROWS + HALF, COLS), BF16),
            jax.ShapeDtypeStruct((1, HALF, COLS), BF16),
        ),
        in_specs=[SMEM] * 4 + [VMEM] * 3,
        out_specs=(VMEM, VMEM, VMEM),
        compiler_params=PARAMS,
        name="mask_inputs",
    )(pos, mask_int, mask_occ, mask_virt, integrals, occ, virt)


def virt_index(pos, offsets):
    z, y, x, core = pos[0], pos[1], pos[2], pos[3]
    first, second = offsets
    own_x = lax.rem(x + jnp.where(core == 0, first, second) + 4, 4)
    own_y = lax.rem(y + jnp.where(core == 0, second, first) + 4, 4)
    tile = own_y * 4 + own_x
    offset = lax.rem(lax.div(tile, 2) - z + 8, 8)
    place = jnp.where(offset < 4, 2 * offset, 2 * (8 - offset) - 1)
    return place + jnp.where(lax.rem(tile, 2) == core, 0, 8)


def chi_rows(first_row, polar, others):
    shape = (8, BLK)
    rows = lax.broadcasted_iota(jnp.int32, shape, 0)
    cols = lax.broadcasted_iota(jnp.int32, shape, 1)
    total = jnp.zeros(shape, F32)
    step = 64
    for p in range(PAIR):
        def body(i, sums):
            at = pl.ds(pl.multiple_of(i * step, step), step)
            left = polar(p, at).astype(F32)
            new = []
            for q, partial in enumerate(sums):
                product = left * others[q](at).astype(F32)
                product = product[:, :BLK] + product[:, BLK:]
                new.append(partial + jnp.sum(product.reshape(step // 8, 8, BLK), axis=0))
            return tuple(new)

        sums = lax.fori_loop(0, ROWS // step, body, tuple(jnp.zeros(shape, F32) for _ in others))
        for q, partial in enumerate(sums):
            total = total + jnp.where((rows == first_row + p) & (cols == q), jnp.sum(partial), 0.0)
    return total


def all_aux(plane, ring, other_plane, other_ring):
    def rows_of(ref, start):
        return lambda at: ref[pl.ds(pl.multiple_of(start + at.start, 64), at.size), :]

    return [
        rows_of(ref, start)
        for a, b in ((plane, ring), (other_plane, other_ring))
        for ref, start in ((a, 0), (a, ROWS), (b, 0), (b, ROWS + HALF))
    ]


def plane_sum(pos, groups, pieces, virt, acc):
    for group, piece in zip(groups, pieces):
        for k, offsets in enumerate(group):
            tile = piece[pl.ds(k * PAIR * ROWS, PAIR * ROWS), :]
            acc[...] += jnp.dot(tile, virt[virt_index(pos, offsets)], preferred_element_type=F32)


def plane_kernel(groups, first, *refs):
    pos, virt = refs[0], refs[1]
    pieces = refs[2:2 + len(groups)]
    out = refs[-1]
    if first:
        out[...] = jnp.zeros_like(out)
    else:
        out[...] = refs[2 + len(groups)][...]
    plane_sum(pos, groups, pieces, virt, out)


def plane_product(pos, virt, groups, pieces, acc=None):
    tiles = sum(len(group) for group in groups)
    return pl.pallas_call(
        functools.partial(plane_kernel, groups, acc is None),
        out_shape=jax.ShapeDtypeStruct((PAIR * ROWS, COLS), F32),
        in_specs=[SMEM] + [VMEM] * (1 + len(groups) + (acc is not None)),
        out_specs=VMEM,
        compiler_params=PARAMS,
        cost_estimate=pl.CostEstimate(
            flops=2 * tiles * PAIR * ROWS * COLS * COLS, bytes_accessed=4 << 20, transcendentals=0
        ),
        name="plane_product",
    )(pos, virt, *pieces, *(() if acc is None else (acc,)))


def plane_half_kernel(groups, pos, virt, top, bottom, acc_in, out, acc):
    acc[...] = acc_in[...]
    plane_sum(pos, groups, (top, bottom), virt, acc)
    out[...] = acc[...].astype(BF16)


def plane_finish(pos, virt, pieces, acc):
    return pl.pallas_call(
        functools.partial(plane_half_kernel, (TOP, BOTTOM)),
        out_shape=jax.ShapeDtypeStruct((PAIR * ROWS, COLS), BF16),
        in_specs=[SMEM] + [VMEM] * 4,
        out_specs=VMEM,
        scratch_shapes=[pltpu.VMEM((PAIR * ROWS, COLS), F32)],
        compiler_params=PARAMS,
        name="plane_finish",
    )(pos, virt, *pieces, acc)


def polar_plane_kernel(pos, virt, top, bottom, acc_in, a0, b0, a1, b1, chi_in, polar_in, polar, chi, acc):
    acc[...] = acc_in[...]
    plane_sum(pos, (TOP, BOTTOM), (top, bottom), virt, acc)
    for p in range(PAIR):
        polar[p] = acc[pl.ds(p * ROWS, ROWS), :].astype(BF16)
    chi[...] = chi_in[...] + chi_rows(PAIR, lambda p, at: polar[p, at, :], all_aux(a0, b0, a1, b1))


def polar_plane(pos, virt, pieces, acc, aux, chi, polar):
    whole = lambda a: pl.BlockSpec(a.shape, lambda i: (0,) * a.ndim)
    operands = (virt, *pieces, acc, *aux, chi)
    return pl.pallas_call(
        polar_plane_kernel,
        grid=(1,),
        out_shape=(
            jax.ShapeDtypeStruct((2 * PAIR, ROWS, COLS), BF16),
            jax.ShapeDtypeStruct((8, BLK), F32),
        ),
        in_specs=[SMEM] + [whole(a) for a in operands] + [pl.BlockSpec(memory_space=pl.ANY)],
        out_specs=(pl.BlockSpec((PAIR, ROWS, COLS), lambda i: (1, 0, 0)), pl.BlockSpec((8, BLK), lambda i: (0, 0))),
        scratch_shapes=[pltpu.VMEM((PAIR * ROWS, COLS), F32)],
        input_output_aliases={len(operands) + 1: 0},
        compiler_params=PARAMS,
        name="polar_plane",
    )(pos, *operands, polar)


def ring_sum(pos, spare, occ, pieces, acc):
    z = pos[0]
    acc[...] = jnp.zeros_like(acc)
    for place, offset in enumerate(RING[:-1]):
        source = lax.rem(z + offset + 8, 8)
        for p in range(PAIR):
            for i in range(ROWS // HALF):
                if place < 7:
                    start = p * (ROWS + spare) + i * HALF
                    piece = pieces[place]
                else:
                    start = p * (spare // 2) + i * HALF
                    piece = pieces[place + p]
                tile = piece[pl.ds(start, HALF), :]
                acc[p] += jnp.dot(occ[source * 2 + i], tile, preferred_element_type=F32)


def ring_kernel(spare, pos, occ, *refs):
    pieces, out, acc = refs[:9], refs[9], refs[10]
    ring_sum(pos, spare, occ, pieces, acc)
    for p in range(PAIR):
        out[pl.ds(p * ROWS, ROWS), :] = acc[p].astype(BF16)


def ring_product(pos, occ, pieces, spare):
    return pl.pallas_call(
        functools.partial(ring_kernel, spare),
        out_shape=jax.ShapeDtypeStruct((PAIR * ROWS, COLS), BF16),
        in_specs=[SMEM] + [VMEM] * 10,
        out_specs=VMEM,
        scratch_shapes=[pltpu.VMEM((PAIR, ROWS, COLS), F32)],
        compiler_params=PARAMS,
        cost_estimate=pl.CostEstimate(flops=2 << 30, bytes_accessed=9 << 20, transcendentals=0),
        name="ring_product",
    )(pos, occ, *pieces)


def polar_ring_kernel(pos, occ, *refs):
    pieces, aux = refs[:9], refs[9:13]
    polar, chi, acc = refs[13:]
    ring_sum(pos, 0, occ, pieces, acc)
    for p in range(PAIR):
        polar[p] = acc[p].astype(BF16)
    chi[...] = chi_rows(0, lambda p, at: polar[p, at, :], all_aux(*aux))


def polar_ring(pos, occ, pieces, aux):
    whole = lambda a: pl.BlockSpec(a.shape, lambda i: (0,) * a.ndim)
    operands = (occ, *pieces, *aux)
    return pl.pallas_call(
        polar_ring_kernel,
        grid=(1,),
        out_shape=(
            jax.ShapeDtypeStruct((2 * PAIR, ROWS, COLS), BF16),
            jax.ShapeDtypeStruct((8, BLK), F32),
        ),
        in_specs=[SMEM] + [whole(a) for a in operands],
        out_specs=(pl.BlockSpec((PAIR, ROWS, COLS), lambda i: (0, 0, 0)), pl.BlockSpec((8, BLK), lambda i: (0, 0))),
        scratch_shapes=[pltpu.VMEM((PAIR, ROWS, COLS), F32)],
        compiler_params=PARAMS,
        cost_estimate=pl.CostEstimate(flops=2 << 30, bytes_accessed=12 << 20, transcendentals=0),
        name="polar_ring",
    )(pos, *operands)


def body(integrals, density_occ, density_virt, mask_int, mask_occ, mask_virt):
    core = lax.axis_index("layer")
    col = lax.axis_index("col")
    pos = jnp.stack([lax.axis_index("row"), col // 4, col % 4, core]).astype(jnp.int32)

    plane_aux, ring_aux, occ_half = mask_inputs(
        pos, mask_int, mask_occ, mask_virt, integrals, density_occ, density_virt
    )
    occ = lax.all_gather(occ_half, ("col", "layer"), axis=0, tiled=True)
    occ = occ.reshape(16, ROWS, COLS)

    plane_parts = gather_plane(plane_aux)
    ring_parts = gather_ring(ring_aux)
    other_plane, other_ring = swap_cores(plane_aux), swap_cores(ring_aux)

    own_virt = jnp.concatenate(
        [part[ROWS:ROWS + HALF] for part in ring_parts[:7]]
        + [ring_parts[7][ROWS:], ring_parts[8][:HALF // 2]],
        axis=0,
    ).reshape(8, HALF, COLS)
    virt = jnp.concatenate([own_virt, swap_cores(own_virt)], axis=0)

    near, before, after, top, bottom = plane_parts
    acc = plane_product(pos, virt, (NEAR, BEFORE, AFTER), (near, before, after))
    half_tensor = plane_finish(pos, virt, (top, bottom), acc)
    occ_first = ring_product(pos, occ, ring_parts, HALF)

    near, before, after, top, bottom = gather_plane(occ_first)
    ring_parts = gather_ring(half_tensor)
    aux = (plane_aux, ring_aux, other_plane, other_ring)
    polar, chi = polar_ring(pos, occ, ring_parts, aux)
    acc = plane_product(pos, virt, (NEAR,), (near,))
    acc = plane_product(pos, virt, (BEFORE, AFTER), (before, after), acc)
    polar, chi = polar_plane(pos, virt, (top, bottom), acc, aux, chi, polar)

    shares = lax.all_to_all(jnp.broadcast_to(chi[None], (128, 8, BLK)), ("row", "col"), 0, 0)
    chi = jnp.sum(shares, axis=0)[:2 * PAIR] * (1.0 / (ROWS * lax.axis_size("row")))
    own, other = chi[:, :4], chi[:, 4:8]
    chi = jnp.where(core == 0, jnp.concatenate([own, other], 1), jnp.concatenate([other, own], 1))
    return polar, chi


def solution(mesh):
    in_specs = (
        P("layer", "row", "col"),
        P("row", "col"),
        P("row", "col"),
        P("layer", "row", "col"),
        P("row", "col"),
        P("row", "col"),
    )
    out_specs = (P("layer", "row", "col"), P("layer", None))
    return jax.shard_map(body, mesh=mesh, in_specs=in_specs, out_specs=out_specs, check_vma=False)
```

```python
import functools

import jax
import jax.numpy as jnp
from jax import lax
from jax.experimental import pallas as pl
from jax.experimental.pallas import tpu as pltpu
from jax.sharding import PartitionSpec as P

BLK = 128
ROWS = 512
COLS = 256
HALF = 256
PAIR = 2
F32 = jnp.float32
BF16 = jnp.bfloat16
VMEM = pl.BlockSpec(memory_space=pltpu.VMEM)
ANY = pl.BlockSpec(memory_space=pl.ANY)
PARAMS = pltpu.CompilerParams(vmem_limit_bytes=48 * 1024 * 1024)


def plane_index(y, x, core):
    return ((y % 4) * 4 + x % 4) * 2 + core


def plane_perm(shift, first):
    pairs = []
    for y in range(4):
        for x in range(4):
            for core in range(2):
                along_x = (core == 0) == first
                to = (y, x + shift) if along_x else (y + shift, x)
                pairs.append((plane_index(y, x, core), plane_index(*to, core)))
    return pairs


def plane_move(value, shift, first):
    return lax.ppermute(value, ("col", "layer"), plane_perm(shift, first))


def ring_move(value, shift):
    return lax.ppermute(value, "row", [(i, (i + shift) % 8) for i in range(8)])


def swap_cores(value):
    return lax.ppermute(value, "layer", [(0, 1), (1, 0)])


PLANE = (
    ((0, 0), (-1, 0)),
    ((1, 0), (2, 0)),
    ((0, -1), (-1, -1)),
    ((1, 1), (2, 1)),
    ((1, -1), (2, -1)),
    ((0, 1), (-1, 1)),
    ((0, 2), (-1, 2)),
    ((1, 2), (2, 2)),
)
NEAR, FAR = PLANE[:6], PLANE[6:]

RING = (0, -1, 1, -2, 2, -3, 3, 4, 4)


def gather_both(plane, ring):
    half = ring.shape[0] // 2
    before = plane_move(plane, 1, True)
    after = plane_move(plane, -1, True)
    up1, down1 = ring_move(ring, 1), ring_move(ring, -1)
    across = plane_move(plane, 2, True)
    top = jnp.concatenate([plane, before], axis=0)
    bottom = jnp.concatenate([after, across], axis=0)
    top_before = plane_move(top, 1, False)
    bottom_after = plane_move(bottom, -1, False)
    bottom_before = plane_move(bottom, 1, False)
    top_after = plane_move(top, -1, False)
    up2, down2 = ring_move(up1, 1), ring_move(down1, -1)
    up3, down3 = ring_move(up2, 1), ring_move(down2, -1)
    top_before, bottom_after, up3, down3 = lax.optimization_barrier((top_before, bottom_after, up3, down3))
    top_far = plane_move(top_before, 1, False)
    bottom_far = plane_move(bottom_after, -1, False)
    up4, down4 = ring_move(up3[:half], 1), ring_move(down3[half:], -1)
    return (
        (top, bottom, top_before, bottom_after, bottom_before, top_after),
        (top_far, bottom_far),
        (ring, up1, down1, up2, down2, up3, down3, up4, down4),
    )


def whole(array):
    return pl.BlockSpec(array.shape, lambda i: (0,) * array.ndim)


def start_all(sources, buffers, sems, first=0):
    copies = [pltpu.make_async_copy(a, b, sems.at[first + i]) for i, (a, b) in enumerate(zip(sources, buffers))]
    for copy in copies:
        copy.start()
    return copies


def buffers_of(arrays):
    return [pltpu.VMEM(a.shape, a.dtype) for a in arrays]


def mask_kernel(mask_int, mask_occ, mask_virt, integrals, occ, virt, plane, ring, occ_half, buf, occ_buf, virt_buf, sems):
    core = lax.axis_index("layer")
    half = pl.ds(pl.multiple_of(core * HALF, HALF), HALF)
    copies = start_all(
        [virt.at[half], occ.at[half]] + [integrals.at[p] for p in range(2 * PAIR)],
        [virt_buf, occ_buf] + [buf.at[p] for p in range(2 * PAIR)],
        sems,
    )

    def masked(ref, row, col, weight):
        block = ref[pl.ds(row, BLK), pl.ds(col, BLK)].astype(F32)
        return (block * jnp.broadcast_to(weight.astype(F32), block.shape)).astype(BF16)

    virt_copy, occ_copy, *aux_copies = copies
    virt_copy.wait()
    occ_copy.wait()
    for i in range(HALF // BLK):
        row = core * (HALF // BLK) + i
        for j in range(COLS // BLK):
            cols = pl.ds(j * BLK, BLK)
            weight = mask_virt[pl.ds(row, 1), pl.ds(j, 1)]
            ring[pl.ds(ROWS + i * BLK, BLK), cols] = masked(virt_buf, i * BLK, j * BLK, weight)
            weight = mask_occ[pl.ds(row, 1), pl.ds(j, 1)]
            occ_half[0, pl.ds(i * BLK, BLK), cols] = masked(occ_buf, i * BLK, j * BLK, weight)
    for p in range(2 * PAIR):
        aux_copies[p].wait()
        for i in range(ROWS // BLK):
            for j in range(COLS // BLK):
                weight = mask_int[p, pl.ds(i, 1), pl.ds(j, 1)]
                block = masked(buf.at[p], i * BLK, j * BLK, weight)
                cols = pl.ds(j * BLK, BLK)
                if p < PAIR:
                    plane[pl.ds(p * ROWS + i * BLK, BLK), cols] = block
                else:
                    ring[pl.ds((p - PAIR) * (ROWS + HALF) + i * BLK, BLK), cols] = block


def mask_inputs(mask_int, mask_occ, mask_virt, integrals, occ, virt):
    outs = (
        jax.ShapeDtypeStruct((PAIR * ROWS, COLS), BF16),
        jax.ShapeDtypeStruct((PAIR * ROWS + HALF, COLS), BF16),
        jax.ShapeDtypeStruct((1, HALF, COLS), BF16),
    )
    return pl.pallas_call(
        mask_kernel,
        grid=(1,),
        out_shape=outs,
        in_specs=[whole(mask_int), whole(mask_occ), whole(mask_virt)] + [ANY] * 3,
        out_specs=tuple(whole(a) for a in outs),
        scratch_shapes=[
            pltpu.VMEM((2 * PAIR, ROWS, COLS), BF16),
            pltpu.VMEM((HALF, COLS), BF16),
            pltpu.VMEM((HALF, COLS), BF16),
            pltpu.SemaphoreType.DMA((2 + 2 * PAIR,)),
        ],
        compiler_params=PARAMS,
        name="mask_inputs",
    )(mask_int, mask_occ, mask_virt, integrals, occ, virt)


def virt_place(offsets):
    z, col, core = lax.axis_index("row"), lax.axis_index("col"), lax.axis_index("layer")
    y, x = lax.div(col, 4), lax.rem(col, 4)
    first, second = offsets
    own_x = lax.rem(x + jnp.where(core == 0, first, second) + 4, 4)
    own_y = lax.rem(y + jnp.where(core == 0, second, first) + 4, 4)
    tile = own_y * 4 + own_x
    offset = lax.rem(lax.div(tile, 2) - z + 8, 8)
    place = jnp.where(offset < 4, 2 * offset, 2 * (8 - offset) - 1)
    return place + jnp.where(lax.rem(tile, 2) == core, 0, 8)


def start_plane(groups, virt, pieces, bufs, virt_buf, sems):
    tiles = [offsets for group in groups for offsets in group]
    piece_copies = start_all(pieces[:1], bufs[:1], sems)
    virt_copies = start_all(
        [virt.at[virt_place(t)] for t in tiles], [virt_buf.at[k] for k in range(len(tiles))], sems, len(groups)
    )
    return piece_copies + start_all(pieces[1:], bufs[1:], sems, 1), virt_copies


def plane_sum(groups, copies, bufs, virt_buf, acc):
    piece_copies, virt_copies = copies
    tile = 0
    for group, copy, buf in zip(groups, piece_copies, bufs):
        copy.wait()
        for k in range(len(group)):
            virt_copies[tile].wait()
            rows = buf[pl.ds(k * PAIR * ROWS, PAIR * ROWS), :]
            acc[...] += jnp.dot(rows, virt_buf[tile], preferred_element_type=F32)
            tile += 1


def plane_kernel(virt, *refs):
    n = len(NEAR)
    pieces, out, bufs, virt_buf, sems = refs[:n], refs[n], refs[n + 1:2 * n + 1], refs[-2], refs[-1]
    copies = start_plane(NEAR, virt, pieces, bufs, virt_buf, sems)
    out[...] = jnp.zeros_like(out)
    plane_sum(NEAR, copies, bufs, virt_buf, out)


def plane_product(virt, pieces):
    return pl.pallas_call(
        plane_kernel,
        out_shape=jax.ShapeDtypeStruct((PAIR * ROWS, COLS), F32),
        in_specs=[ANY] * (1 + len(NEAR)),
        out_specs=VMEM,
        scratch_shapes=buffers_of(pieces)
        + [pltpu.VMEM((12, HALF, COLS), BF16), pltpu.SemaphoreType.DMA((len(NEAR) + 12,))],
        compiler_params=PARAMS,
        cost_estimate=pl.CostEstimate(flops=24 * PAIR * ROWS * COLS * COLS, bytes_accessed=8 << 20, transcendentals=0),
        name="plane_product",
    )(virt, *pieces)


def plane_finish_kernel(virt, top, bottom, acc_in, out, top_buf, bottom_buf, virt_buf, acc, sems):
    bufs = (top_buf, bottom_buf)
    copies = start_plane(FAR, virt, (top, bottom), bufs, virt_buf, sems)
    acc[...] = acc_in[...]
    plane_sum(FAR, copies, bufs, virt_buf, acc)
    out[...] = acc[...].astype(BF16)


def plane_finish(virt, pieces, acc):
    return pl.pallas_call(
        plane_finish_kernel,
        out_shape=jax.ShapeDtypeStruct((PAIR * ROWS, COLS), BF16),
        in_specs=[ANY] * 3 + [VMEM],
        out_specs=VMEM,
        scratch_shapes=buffers_of(pieces)
        + [pltpu.VMEM((4, HALF, COLS), BF16), pltpu.VMEM((PAIR * ROWS, COLS), F32), pltpu.SemaphoreType.DMA((6,))],
        compiler_params=PARAMS,
        cost_estimate=pl.CostEstimate(flops=8 * PAIR * ROWS * COLS * COLS, bytes_accessed=4 << 20, transcendentals=0),
        name="plane_finish",
    )(virt, *pieces, acc)


def chi_rows(first_row, polar, others):
    shape = (8, BLK)
    step = 32

    def add_rows(i, sums):
        at = pl.multiple_of(i * step, step)
        left = [polar[p, pl.ds(at, step), :].astype(F32) for p in range(PAIR)]
        new = []
        for q, (ref, start) in enumerate(others):
            right = ref[pl.ds(pl.multiple_of(start + at, step), step), :].astype(F32)
            for p in range(PAIR):
                product = left[p] * right
                product = product[:, :BLK] + product[:, BLK:]
                new.append(sums[q * PAIR + p] + jnp.sum(product.reshape(step // 8, 8, BLK), axis=0))
        return tuple(new)

    zeros = tuple(jnp.zeros(shape, F32) for _ in range(PAIR * len(others)))
    sums = lax.fori_loop(0, ROWS // step, add_rows, zeros)
    rows = lax.broadcasted_iota(jnp.int32, shape, 0)
    cols = lax.broadcasted_iota(jnp.int32, shape, 1)
    total = jnp.zeros(shape, F32)
    for k, partial in enumerate(sums):
        q, p = divmod(k, PAIR)
        total = total + jnp.where((rows == first_row + p) & (cols == q), jnp.sum(partial), 0.0)
    return total


def aux_rows(plane, ring, other_plane, other_ring):
    return [
        (ref, start)
        for a, b in ((plane, ring), (other_plane, other_ring))
        for ref, start in ((a, 0), (a, ROWS), (b, 0), (b, ROWS + HALF))
    ]


def polar_plane_kernel(virt, top, bottom, a0, b0, a1, b1, polar_in, acc_in, chi_in, polar, chi,
                       top_buf, bottom_buf, virt_buf, acc, c0, d0, c1, d1, sems):
    bufs = (top_buf, bottom_buf)
    copies = start_plane(FAR, virt, (top, bottom), bufs, virt_buf, sems)
    aux = (c0, d0, c1, d1)
    aux_copies = start_all((a0, b0, a1, b1), aux, sems, 6)
    acc[...] = acc_in[...]
    plane_sum(FAR, copies, bufs, virt_buf, acc)
    for p in range(PAIR):
        polar[p] = acc[pl.ds(p * ROWS, ROWS), :].astype(BF16)
    for copy in aux_copies:
        copy.wait()
    chi[...] = chi_in[...] + chi_rows(PAIR, polar, aux_rows(*aux))


def polar_plane(virt, pieces, acc, aux, chi, polar):
    return pl.pallas_call(
        polar_plane_kernel,
        grid=(1,),
        out_shape=(
            jax.ShapeDtypeStruct((2 * PAIR, ROWS, COLS), BF16),
            jax.ShapeDtypeStruct((8, BLK), F32),
        ),
        in_specs=[ANY] * 8 + [whole(acc), whole(chi)],
        out_specs=(pl.BlockSpec((PAIR, ROWS, COLS), lambda i: (1, 0, 0)), whole(chi)),
        scratch_shapes=buffers_of(pieces)
        + [pltpu.VMEM((4, HALF, COLS), BF16), pltpu.VMEM((PAIR * ROWS, COLS), F32)]
        + buffers_of(aux) + [pltpu.SemaphoreType.DMA((10,))],
        input_output_aliases={7: 0},
        compiler_params=PARAMS,
        cost_estimate=pl.CostEstimate(flops=8 * PAIR * ROWS * COLS * COLS, bytes_accessed=8 << 20, transcendentals=0),
        name="polar_plane",
    )(virt, *pieces, *aux, polar, acc, chi)


def start_ring(occ, pieces, bufs, occ_buf, sems):
    z = lax.axis_index("row")
    occ_copies, piece_copies = [], []
    for place in range(8):
        source = lax.rem(z + RING[place] + 8, 8)
        occ_copies += start_all([occ.at[pl.ds(source * 2, 2)]], [occ_buf.at[pl.ds(place * 2, 2)]], sems, place)
        piece_copies += start_all([pieces[place]], [bufs[place]], sems, 8 + place)
    return occ_copies, piece_copies + start_all([pieces[8]], [bufs[8]], sems, 16)


def ring_sum(spare, copies, bufs, occ_buf, acc):
    occ_copies, piece_copies = copies
    for place in range(8):
        occ_copies[place].wait()
        piece_copies[place].wait()
        if place == 7:
            piece_copies[8].wait()
        for p in range(PAIR):
            if place < 7:
                piece, start = bufs[place], p * (ROWS + spare)
            else:
                piece, start = bufs[place + p], p * (spare // 2)
            part = jnp.dot(occ_buf[place * 2], piece[pl.ds(start, HALF), :], preferred_element_type=F32)
            part += jnp.dot(occ_buf[place * 2 + 1], piece[pl.ds(start + HALF, HALF), :], preferred_element_type=F32)
            acc[p] = part if place == 0 else acc[p] + part


def ring_kernel(spare, occ, *refs):
    pieces, out, bufs, occ_buf, acc, sems = refs[:9], refs[9], refs[10:19], refs[19], refs[20], refs[21]
    copies = start_ring(occ, pieces, bufs, occ_buf, sems)
    ring_sum(spare, copies, bufs, occ_buf, acc)
    for p in range(PAIR):
        out[pl.ds(p * ROWS, ROWS), :] = acc[p].astype(BF16)


def ring_product(occ, pieces, spare):
    return pl.pallas_call(
        functools.partial(ring_kernel, spare),
        out_shape=jax.ShapeDtypeStruct((PAIR * ROWS, COLS), BF16),
        in_specs=[ANY] * 10,
        out_specs=VMEM,
        scratch_shapes=buffers_of(pieces)
        + buffers_of((occ,)) + [pltpu.VMEM((PAIR, ROWS, COLS), F32), pltpu.SemaphoreType.DMA((17,))],
        compiler_params=PARAMS,
        cost_estimate=pl.CostEstimate(flops=2 << 30, bytes_accessed=9 << 20, transcendentals=0),
        name="ring_product",
    )(occ, *pieces)


def polar_ring_kernel(occ, *refs):
    pieces, aux, polar, chi = refs[:9], refs[9:13], refs[13], refs[14]
    bufs, aux_bufs, occ_buf, acc, sems = refs[15:24], refs[24:28], refs[28], refs[29], refs[30]
    copies = start_ring(occ, pieces, bufs, occ_buf, sems)
    aux_copies = start_all(aux, aux_bufs, sems, 17)
    ring_sum(0, copies, bufs, occ_buf, acc)
    for p in range(PAIR):
        polar[p] = acc[p].astype(BF16)
    for copy in aux_copies:
        copy.wait()
    chi[...] = chi_rows(0, polar, aux_rows(*aux_bufs))


def polar_ring(occ, pieces, aux):
    return pl.pallas_call(
        polar_ring_kernel,
        grid=(1,),
        out_shape=(
            jax.ShapeDtypeStruct((2 * PAIR, ROWS, COLS), BF16),
            jax.ShapeDtypeStruct((8, BLK), F32),
        ),
        in_specs=[ANY] * 14,
        out_specs=(pl.BlockSpec((PAIR, ROWS, COLS), lambda i: (0, 0, 0)), pl.BlockSpec((8, BLK), lambda i: (0, 0))),
        scratch_shapes=buffers_of(pieces) + buffers_of(aux)
        + buffers_of((occ,)) + [pltpu.VMEM((PAIR, ROWS, COLS), F32), pltpu.SemaphoreType.DMA((21,))],
        compiler_params=PARAMS,
        cost_estimate=pl.CostEstimate(flops=2 << 30, bytes_accessed=12 << 20, transcendentals=0),
        name="polar_ring",
    )(occ, *pieces, *aux)


def body(integrals, density_occ, density_virt, mask_int, mask_occ, mask_virt):
    core = lax.axis_index("layer")
    plane_aux, ring_aux, occ_half = mask_inputs(
        mask_int, mask_occ, mask_virt, integrals, density_occ, density_virt
    )
    occ = lax.all_gather(occ_half, ("col", "layer"), axis=0, tiled=True)
    occ = occ.reshape(16, ROWS, COLS)

    near, far, ring = gather_both(plane_aux, ring_aux)
    own_virt = jnp.concatenate(
        [part[ROWS:ROWS + HALF] for part in ring[:7]] + [ring[7][ROWS:], ring[8][:HALF // 2]], axis=0
    ).reshape(8, HALF, COLS)
    virt = jnp.concatenate([own_virt, swap_cores(own_virt)], axis=0)
    occ_first = ring_product(occ, ring, HALF)
    half_tensor = plane_finish(virt, far, plane_product(virt, near))

    near, far, ring = gather_both(occ_first, half_tensor)
    aux = (plane_aux, ring_aux, swap_cores(plane_aux), swap_cores(ring_aux))
    polar, chi = polar_ring(occ, ring, aux)
    polar, chi = polar_plane(virt, far, plane_product(virt, near), aux, chi, polar)

    shares = lax.all_to_all(jnp.broadcast_to(chi[None], (128, 8, BLK)), ("row", "col"), 0, 0)
    chi = jnp.sum(shares, axis=0)[:2 * PAIR] * (1.0 / (ROWS * lax.axis_size("row")))
    own, other = chi[:, :4], chi[:, 4:8]
    chi = jnp.where(core == 0, jnp.concatenate([own, other], 1), jnp.concatenate([other, own], 1))
    return polar, chi


def solution(mesh):
    in_specs = (
        P("layer", "row", "col"),
        P("row", "col"),
        P("row", "col"),
        P("layer", "row", "col"),
        P("row", "col"),
        P("row", "col"),
    )
    out_specs = (P("layer", "row", "col"), P("layer", None))
    return jax.shard_map(body, mesh=mesh, in_specs=in_specs, out_specs=out_specs, check_vma=False)
```

```python
import functools

import jax
import jax.numpy as jnp
from jax import lax
from jax.experimental import pallas as pl
from jax.experimental.pallas import tpu as pltpu
from jax.sharding import PartitionSpec as P

BLK = 128
ROWS = 512
COLS = 256
HALF = 256
PAIR = 2
AUX = 2 * PAIR
F32 = jnp.float32
BF16 = jnp.bfloat16
VMEM = pl.BlockSpec(memory_space=pltpu.VMEM)
HBM = pl.BlockSpec(memory_space=pltpu.HBM)
PARAMS = pltpu.CompilerParams(vmem_limit_bytes=48 * 1024 * 1024)


def plane_index(y, x, core):
    return ((y % 4) * 4 + x % 4) * 2 + core


def plane_perm(shift, first):
    pairs = []
    for y in range(4):
        for x in range(4):
            for core in range(2):
                along_x = (core == 0) == first
                to = (y, x + shift) if along_x else (y + shift, x)
                pairs.append((plane_index(y, x, core), plane_index(*to, core)))
    return pairs


def plane_move(value, shift, first):
    return lax.ppermute(value, ("col", "layer"), plane_perm(shift, first))


def ring_move(value, shift):
    return lax.ppermute(value, "row", [(i, (i + shift) % 8) for i in range(8)])


def swap_cores(value):
    return lax.ppermute(value, "layer", [(0, 1), (1, 0)])


PLANE = (
    ((0, 0), (-1, 0)),
    ((1, 0), (2, 0)),
    ((0, -1), (-1, -1)),
    ((1, 1), (2, 1)),
    ((1, -1), (2, -1), (0, 2), (-1, 2)),
    ((0, 1), (-1, 1), (1, 2), (2, 2)),
)
PLANE_NEAR, PLANE_FAR = (0, 1, 2, 3), (4, 5)

RING = (0, -1, 1, -2, 2, -3, 3, 4)
RING_NEAR, RING_FAR = (0, 1, 2, 3, 4), (5, 6, 7)


def gather_both(plane, ring, early=None):
    half = ring.shape[0] // 2
    before, after = plane_move(plane, 1, True), plane_move(plane, -1, True)
    up1, down1 = ring_move(ring, 1), ring_move(ring, -1)
    across = plane_move(plane, 2, True)
    before, after, across, up1, down1 = lax.optimization_barrier((before, after, across, up1, down1))
    top = jnp.concatenate([plane, before], axis=0)
    bottom = jnp.concatenate([after, across], axis=0)
    top_before, bottom_after = plane_move(top, 1, False), plane_move(bottom, -1, False)
    up2, down2 = ring_move(up1, 1), ring_move(down1, -1)
    top_before, bottom_after, up2, down2 = lax.optimization_barrier((top_before, bottom_after, up2, down2))
    last_before = plane_move(jnp.concatenate([bottom, top_before], axis=0), 1, False)
    last_after = plane_move(jnp.concatenate([top, bottom_after], axis=0), -1, False)
    up3, down3 = ring_move(up2, 1), ring_move(down2, -1)
    near = (top, bottom, top_before, bottom_after)
    result = None
    if early is not None:
        result = early(near, (ring, up1, down1, up2, down2))
        up3, down3, result = lax.optimization_barrier((up3, down3, result))
    up4, down4 = ring_move(up3[:half], 1), ring_move(down3[half:], -1)
    return near + (last_before, last_after), (ring, up1, down1, up2, down2, up3, down3, up4, down4), result


def whole(array):
    return pl.BlockSpec(array.shape, lambda i: (0,) * array.ndim)


def buffers_of(arrays):
    return [pltpu.VMEM(a.shape, a.dtype) for a in arrays]


def start_all(sources, buffers, sems, first=0):
    copies = [pltpu.make_async_copy(a, b, sems.at[first + i]) for i, (a, b) in enumerate(zip(sources, buffers))]
    for copy in copies:
        copy.start()
    return copies


def mask_kernel(mask_int, mask_occ, mask_virt, integrals, occ, virt, plane, ring, occ_half, aux, buf, occ_buf, virt_buf, sems):
    core = lax.axis_index("layer")
    half = pl.ds(pl.multiple_of(core * HALF, HALF), HALF)
    copies = start_all(
        [virt.at[half], occ.at[half]] + [integrals.at[p] for p in range(AUX)],
        [virt_buf, occ_buf] + [buf.at[p] for p in range(AUX)],
        sems,
    )

    def masked(ref, row, col, weight):
        block = ref[pl.ds(row, BLK), pl.ds(col, BLK)].astype(F32)
        return (block * jnp.broadcast_to(weight.astype(F32), block.shape)).astype(BF16)

    def half_weight(mask, i, j):
        low, high = mask[pl.ds(j, 1), pl.ds(i, 1)], mask[pl.ds(j, 1), pl.ds(HALF // BLK + i, 1)]
        return jnp.where(core == 0, low, high)

    virt_copy, occ_copy, *aux_copies = copies
    virt_copy.wait()
    occ_copy.wait()
    for i in range(HALF // BLK):
        for j in range(COLS // BLK):
            cols = pl.ds(j * BLK, BLK)
            weight = half_weight(mask_virt, i, j)
            ring[pl.ds(ROWS + i * BLK, BLK), cols] = masked(virt_buf, i * BLK, j * BLK, weight)
            weight = half_weight(mask_occ, i, j)
            occ_half[0, pl.ds(i * BLK, BLK), cols] = masked(occ_buf, i * BLK, j * BLK, weight)
    for p in range(AUX):
        aux_copies[p].wait()
        for i in range(ROWS // BLK):
            for j in range(COLS // BLK):
                block = masked(buf.at[p], i * BLK, j * BLK, mask_int[p, pl.ds(j, 1), pl.ds(i, 1)])
                cols = pl.ds(j * BLK, BLK)
                aux[p, pl.ds(i * BLK, BLK), cols] = block
                if p < PAIR:
                    plane[pl.ds(p * ROWS + i * BLK, BLK), cols] = block
                else:
                    ring[pl.ds((p - PAIR) * (ROWS + HALF) + i * BLK, BLK), cols] = block


def mask_inputs(mask_int, mask_occ, mask_virt, integrals, occ, virt):
    outs = (
        jax.ShapeDtypeStruct((PAIR * ROWS, COLS), BF16),
        jax.ShapeDtypeStruct((PAIR * ROWS + HALF, COLS), BF16),
        jax.ShapeDtypeStruct((1, HALF, COLS), BF16),
        jax.ShapeDtypeStruct((AUX, ROWS, COLS), BF16),
    )
    masks = (mask_int.transpose(0, 2, 1), mask_occ.T, mask_virt.T)
    return pl.pallas_call(
        mask_kernel,
        grid=(1,),
        out_shape=outs,
        in_specs=[whole(a) for a in masks] + [HBM] * 3,
        out_specs=tuple(whole(a) for a in outs),
        scratch_shapes=[
            pltpu.VMEM((AUX, ROWS, COLS), BF16),
            pltpu.VMEM((HALF, COLS), BF16),
            pltpu.VMEM((HALF, COLS), BF16),
            pltpu.SemaphoreType.DMA((2 + AUX,)),
        ],
        compiler_params=PARAMS,
        name="mask_inputs",
    )(*masks, integrals, occ, virt)


def virt_place(offsets):
    z, col, core = lax.axis_index("row"), lax.axis_index("col"), lax.axis_index("layer")
    y, x = lax.div(col, 4), lax.rem(col, 4)
    first, second = offsets
    own_x = lax.rem(x + jnp.where(core == 0, first, second) + 4, 4)
    own_y = lax.rem(y + jnp.where(core == 0, second, first) + 4, 4)
    tile = own_y * 4 + own_x
    offset = lax.rem(lax.div(tile, 2) - z + 8, 8)
    place = jnp.where(offset < 4, 2 * offset, 2 * (8 - offset) - 1)
    return place + jnp.where(lax.rem(tile, 2) == core, 0, 8)


class PlaneSum:
    def __init__(self, arrays):
        self.groups = [PLANE[a] for a in arrays]
        self.tiles = [offsets for group in self.groups for offsets in group]
        self.sems = len(arrays) + len(self.tiles)

    def scratch(self, pieces):
        return buffers_of(pieces) + [pltpu.VMEM((len(self.tiles), HALF, COLS), BF16)]

    def start(self, virt, pieces, bufs, sems, first):
        *self.bufs, self.virt_buf = bufs
        piece_copies = start_all(pieces[:1], self.bufs[:1], sems, first)
        self.virt_copies = start_all(
            [virt.at[virt_place(t)] for t in self.tiles],
            [self.virt_buf.at[k] for k in range(len(self.tiles))],
            sems,
            first + len(pieces),
        )
        self.piece_copies = piece_copies + start_all(pieces[1:], self.bufs[1:], sems, first + 1)

    def add(self, acc, fresh):
        tile = 0
        for group, copy, buf in zip(self.groups, self.piece_copies, self.bufs):
            copy.wait()
            for k in range(0, len(group), 2):
                self.virt_copies[tile].wait()
                self.virt_copies[tile + 1].wait()
                for p in range(PAIR):
                    part = jnp.zeros((ROWS, COLS), F32)
                    for i in range(2):
                        rows = buf[pl.ds(((k + i) * PAIR + p) * ROWS, ROWS), :]
                        part += jnp.dot(rows, self.virt_buf[tile + i], preferred_element_type=F32)
                    at = pl.ds(p * ROWS, ROWS)
                    acc[at, :] = part if fresh and tile == 0 else acc[at, :] + part
                tile += 2


class RingSum:
    def __init__(self, places, spare):
        self.places, self.spare = places, spare
        self.count = len(places) + (7 in places)
        self.sems = len(places) + self.count

    def scratch(self, pieces):
        return buffers_of(pieces) + [pltpu.VMEM((2 * len(self.places), ROWS, COLS), BF16)]

    def start(self, occ, pieces, bufs, sems, first):
        *self.bufs, self.occ_buf = bufs
        z = lax.axis_index("row")
        self.occ_copies, self.piece_copies = [], []
        for k, place in enumerate(self.places):
            source = lax.rem(z + RING[place] + 8, 8)
            self.occ_copies += start_all(
                [occ.at[pl.ds(source * 2, 2)]], [self.occ_buf.at[pl.ds(k * 2, 2)]], sems, first + k
            )
            self.piece_copies += start_all([pieces[k]], [self.bufs[k]], sems, first + len(self.places) + k)
        for k in range(len(self.places), self.count):
            self.piece_copies += start_all([pieces[k]], [self.bufs[k]], sems, first + len(self.places) + k)

    def add(self, acc, fresh):
        for k, place in enumerate(self.places):
            self.occ_copies[k].wait()
            self.piece_copies[k].wait()
            if place == 7:
                self.piece_copies[k + 1].wait()
            for p in range(PAIR):
                if place < 7:
                    piece, start = self.bufs[k], p * (ROWS + self.spare)
                else:
                    piece, start = self.bufs[k + p], p * (self.spare // 2)
                part = jnp.dot(self.occ_buf[2 * k], piece[pl.ds(start, HALF), :], preferred_element_type=F32)
                part += jnp.dot(
                    self.occ_buf[2 * k + 1], piece[pl.ds(start + HALF, HALF), :], preferred_element_type=F32
                )
                at = pl.ds(p * ROWS, ROWS)
                acc[at, :] = part if fresh and k == 0 else acc[at, :] + part


def product_kernel(job, factor, *refs):
    n = (len(refs) - 3) // 2
    pieces, out, bufs, acc, sems = refs[:n], refs[n], refs[n + 1:-2], refs[-2], refs[-1]
    job.start(factor, pieces, bufs, sems, 0)
    job.add(acc, True)
    out[...] = acc[...].astype(out.dtype)


def product(name, job, factor, pieces, dtype):
    return pl.pallas_call(
        functools.partial(product_kernel, job),
        out_shape=jax.ShapeDtypeStruct((PAIR * ROWS, COLS), dtype),
        in_specs=[HBM] * (1 + len(pieces)),
        out_specs=VMEM,
        scratch_shapes=job.scratch(pieces)
        + [pltpu.VMEM((PAIR * ROWS, COLS), F32), pltpu.SemaphoreType.DMA((job.sems,))],
        compiler_params=PARAMS,
        cost_estimate=pl.CostEstimate(flops=2 << 30, bytes_accessed=9 << 20, transcendentals=0),
        name=name,
    )(factor, *pieces)


CHUNK = 32


def chi_tile(polar, aux):
    count = aux.shape[0]

    def add_rows(i, total):
        at = pl.ds(pl.multiple_of(i * CHUNK, CHUNK), CHUNK)
        left = jnp.concatenate([polar[p, at, :] for p in range(AUX)], axis=0)
        right = jnp.concatenate([aux[q, at, :] for q in range(count)], axis=0)
        return total + lax.dot_general(left, right, (((1,), (1,)), ((), ())), preferred_element_type=F32)

    shape = (AUX * CHUNK, count * CHUNK)
    total = lax.fori_loop(0, ROWS // CHUNK, add_rows, jnp.zeros(shape, F32), unroll=4)
    rows = lax.broadcasted_iota(jnp.int32, shape, 0)
    cols = lax.broadcasted_iota(jnp.int32, shape, 1)
    total = jnp.where(lax.rem(rows, CHUNK) == lax.rem(cols, CHUNK), total, 0.0)
    sums = [jnp.sum(total[p * CHUNK:(p + 1) * CHUNK], axis=0, keepdims=True) for p in range(AUX)]
    sums = jnp.concatenate(sums + [jnp.zeros((8 - AUX, shape[1]), F32)], axis=0)
    cols = lax.broadcasted_iota(jnp.int32, (8, BLK), 1)
    result = jnp.zeros((8, BLK), F32)
    for q in range(count):
        group = lax.broadcasted_iota(jnp.int32, sums.shape, 1) // CHUNK == q
        value = jnp.sum(jnp.where(group, sums, 0.0), axis=1, keepdims=True)
        result = jnp.where(cols == q, value, result)
    return result


def polar_kernel(plane_job, ring_job, virt, occ, *refs):
    n, m = 2, ring_job.count
    plane_pieces, ring_pieces, aux = refs[:n], refs[n:n + m], refs[n + m]
    plane_in, ring_in, polar, chi = refs[n + m + 1:n + m + 5]
    scratch = refs[n + m + 5:]
    plane_bufs, ring_bufs = scratch[:n + 1], scratch[n + 1:n + m + 2]
    aux_buf, plane_acc, ring_acc, sems = scratch[n + m + 2:]
    copies = start_all((plane_in, ring_in), (plane_acc, ring_acc), sems)
    ring_job.start(occ, ring_pieces, ring_bufs, sems, 3)
    plane_job.start(virt, plane_pieces, plane_bufs, sems, 3 + ring_job.sems)
    copies += start_all((aux,), (aux_buf,), sems, 2)
    copies[1].wait()
    ring_job.add(ring_acc, False)
    for p in range(PAIR):
        polar[p] = ring_acc[pl.ds(p * ROWS, ROWS), :].astype(BF16)
    copies[0].wait()
    plane_job.add(plane_acc, False)
    for p in range(PAIR):
        polar[PAIR + p] = plane_acc[pl.ds(p * ROWS, ROWS), :].astype(BF16)
    copies[2].wait()
    tile = chi_tile(polar, aux_buf)
    for i in range(chi.shape[0]):
        chi[i] = tile


def polar_product(virt, occ, plane_pieces, ring_pieces, aux, plane_acc, ring_acc):
    plane_job, ring_job = PlaneSum(PLANE_FAR), RingSum(RING_FAR, 0)
    outs = (jax.ShapeDtypeStruct((AUX, ROWS, COLS), BF16), jax.ShapeDtypeStruct((128, 8, BLK), F32))
    operands = (virt, occ, *plane_pieces, *ring_pieces, aux, plane_acc, ring_acc)
    return pl.pallas_call(
        functools.partial(polar_kernel, plane_job, ring_job),
        grid=(1,),
        out_shape=outs,
        in_specs=[HBM] * len(operands),
        out_specs=tuple(whole(a) for a in outs),
        scratch_shapes=plane_job.scratch(plane_pieces)
        + ring_job.scratch(ring_pieces)
        + buffers_of((aux, plane_acc, ring_acc))
        + [pltpu.SemaphoreType.DMA((3 + plane_job.sems + ring_job.sems,))],
        compiler_params=PARAMS,
        cost_estimate=pl.CostEstimate(flops=2 << 30, bytes_accessed=14 << 20, transcendentals=0),
        name="polar_product",
    )(*operands)


def body(integrals, density_occ, density_virt, mask_int, mask_occ, mask_virt):
    plane_aux, ring_aux, occ_half, own_aux = mask_inputs(
        mask_int, mask_occ, mask_virt, integrals, density_occ, density_virt
    )
    occ = lax.all_gather(occ_half, ("col", "layer"), axis=0, tiled=True)
    occ = occ.reshape(16, ROWS, COLS)

    plane, ring, _ = gather_both(plane_aux, ring_aux)
    own_virt = jnp.concatenate(
        [part[ROWS:ROWS + HALF] for part in ring[:7]] + [ring[7][ROWS:], ring[8][:HALF // 2]], axis=0
    ).reshape(8, HALF, COLS)
    virt = jnp.concatenate([own_virt, swap_cores(own_virt)], axis=0)
    occ_first = product("occ_first", RingSum(RING_NEAR + RING_FAR, HALF), occ, ring, BF16)
    plane, virt, occ_first = lax.optimization_barrier((plane, virt, occ_first))
    half_tensor = product("half_tensor", PlaneSum(PLANE_NEAR + PLANE_FAR), virt, plane, BF16)

    def early(plane, ring):
        return (
            product("plane_near", PlaneSum(PLANE_NEAR), virt, plane, F32),
            product("ring_near", RingSum(RING_NEAR, 0), occ, ring, F32),
        )

    aux, occ_first = lax.optimization_barrier((own_aux, occ_first))
    aux = lax.all_gather(aux, "layer", axis=0, tiled=True)
    plane, ring, (plane_acc, ring_acc) = gather_both(occ_first, half_tensor, early)
    polar, chi = polar_product(virt, occ, plane[4:], ring[5:], aux, plane_acc, ring_acc)

    shares = lax.all_to_all(chi, ("row", "col"), 0, 0)
    chi = jnp.sum(shares, axis=0)[:AUX, :2 * AUX] * (1.0 / (ROWS * lax.axis_size("row")))
    return polar, chi


def solution(mesh):
    in_specs = (
        P("layer", "row", "col"),
        P("row", "col"),
        P("row", "col"),
        P("layer", "row", "col"),
        P("row", "col"),
        P("row", "col"),
    )
    out_specs = (P("layer", "row", "col"), P("layer", None))
    return jax.shard_map(body, mesh=mesh, in_specs=in_specs, out_specs=out_specs, check_vma=False)
```

```python
import functools

import jax
import jax.numpy as jnp
from jax import lax
from jax.experimental import pallas as pl
from jax.experimental.pallas import tpu as pltpu
from jax.sharding import PartitionSpec as P

BLK = 128
ROWS = 512
COLS = 256
HALF = 256
PAIR = 2
AUX = 2 * PAIR
STRIDE = PAIR * ROWS + HALF
F32 = jnp.float32
BF16 = jnp.bfloat16
HBM = pl.BlockSpec(memory_space=pltpu.HBM)
PARAMS = pltpu.CompilerParams(vmem_limit_bytes=60 * 1024 * 1024)


def plane_index(y, x, core):
    return ((y % 4) * 4 + x % 4) * 2 + core


def plane_perm(shift, first):
    pairs = []
    for y in range(4):
        for x in range(4):
            for core in range(2):
                along_x = (core == 0) == first
                to = (y, x + shift) if along_x else (y + shift, x)
                pairs.append((plane_index(y, x, core), plane_index(*to, core)))
    return pairs


def plane_move(value, shift, first):
    return lax.ppermute(value, ("col", "layer"), plane_perm(shift, first))


def swap_cores(value):
    return lax.ppermute(value, "layer", [(0, 1), (1, 0)])


PLANE = (
    ((0, 0), (-1, 0)),
    ((1, 0), (2, 0)),
    ((0, -1), (-1, -1)),
    ((0, 1), (-1, 1)),
    ((1, -1), (2, -1)),
    ((1, 1), (2, 1)),
    ((0, 2), (-1, 2)),
    ((1, 2), (2, 2)),
)


def gather_plane(plane):
    rows = plane.shape[0]
    half = rows // 2
    before, behind = plane_move(plane, 1, True), plane_move(plane, -1, True)
    low, high = plane_move(before[:half], 1, True), plane_move(behind[half:], -1, True)
    top, = pack((plane, before), ((0, 0, rows, 0, 0), (1, 0, rows, 0, rows)), (2 * rows,))
    top_before, top_behind = plane_move(top, 1, False), plane_move(top, -1, False)
    bottom, = pack(
        (behind, low, high),
        ((0, 0, rows, 0, 0), (1, 0, half, 0, rows), (2, 0, half, 0, rows + half)),
        (2 * rows,),
    )
    bottom_before, bottom_behind = plane_move(bottom, 1, False), plane_move(bottom, -1, False)
    top_before, top_behind, bottom_before, bottom_behind = lax.optimization_barrier(
        (top_before, top_behind, bottom_before, bottom_behind)
    )
    top_far, bottom_far = plane_move(top_before, 1, False), plane_move(bottom_behind, -1, False)
    return top, bottom, top_before, top_behind, bottom_before, bottom_behind, top_far, bottom_far


def buffers_of(arrays):
    return [pltpu.VMEM(a.shape, a.dtype) for a in arrays]


def start_all(sources, buffers, sems, first=0):
    copies = [pltpu.make_async_copy(a, b, sems.at[first + i]) for i, (a, b) in enumerate(zip(sources, buffers))]
    for copy in copies:
        copy.start()
    return copies


def pack_kernel(moves, count, *refs):
    sources, outs, buf, sems = refs[:count], refs[count:-2], refs[-2], refs[-1]
    loads, stores, at = [], [], 0
    for k, (i, start, rows, o, to) in enumerate(moves):
        part = buf.at[pl.ds(at, rows)]
        loads.append(pltpu.make_async_copy(sources[i].at[pl.ds(start, rows)], part, sems.at[0, k]))
        stores.append(pltpu.make_async_copy(part, outs[o].at[pl.ds(to, rows)], sems.at[1, k]))
        at += rows
    for load in loads:
        load.start()
    for load, store in zip(loads, stores):
        load.wait()
        store.start()
    for store in stores:
        store.wait()


def pack(sources, moves, out_rows):
    return pl.pallas_call(
        functools.partial(pack_kernel, moves, len(sources)),
        out_shape=tuple(jax.ShapeDtypeStruct((rows, COLS), BF16) for rows in out_rows),
        in_specs=[HBM] * len(sources),
        out_specs=(HBM,) * len(out_rows),
        scratch_shapes=[
            pltpu.VMEM((sum(move[2] for move in moves), COLS), BF16),
            pltpu.SemaphoreType.DMA((2, len(moves))),
        ],
        compiler_params=PARAMS,
        cost_estimate=pl.CostEstimate(flops=0, bytes_accessed=4 << 20, transcendentals=0),
        name="pack",
    )(*sources)


def mask_kernel(mask_int, mask_occ, mask_virt, integrals, occ, virt, plane, ring, aux,
                int_buf, occ_buf, virt_buf, int_weight, occ_weight, virt_weight, load, store):
    core = lax.axis_index("layer")
    half = pl.ds(pl.multiple_of(core * HALF, HALF), HALF)
    weights = start_all((mask_int, mask_occ, mask_virt), (int_weight, occ_weight, virt_weight), load)
    loads = start_all([integrals.at[p] for p in range(AUX)], [int_buf.at[p] for p in range(AUX)], load, 3)
    loads += start_all([virt.at[half], occ.at[half]], [virt_buf, occ_buf], load, 3 + AUX)

    def mask(ref, weight, block_rows):
        for i in range(block_rows):
            for j in range(COLS // BLK):
                at = pl.ds(i * BLK, BLK), pl.ds(j * BLK, BLK)
                block = ref[at].astype(F32)
                ref[at] = (block * jnp.broadcast_to(weight(i, j).astype(F32), block.shape)).astype(BF16)

    def half_weight(ref):
        def weight(i, j):
            low, high = ref[pl.ds(j, 1), pl.ds(i, 1)], ref[pl.ds(j, 1), pl.ds(HALF // BLK + i, 1)]
            return jnp.where(core == 0, low, high)

        return weight

    for copy in weights:
        copy.wait()
    stores = []
    for p in range(AUX):
        loads[p].wait()
        mask(int_buf.at[p], lambda i, j: int_weight[p, pl.ds(j, 1), pl.ds(i, 1)], ROWS // BLK)
        if p < PAIR:
            to = plane.at[pl.ds(p * ROWS, ROWS)]
        else:
            to = ring.at[pl.ds((p - PAIR) * (ROWS + HALF), ROWS)]
        stores += start_all([int_buf.at[p], int_buf.at[p]], [to, aux.at[p]], store, 2 * p)
    loads[AUX].wait()
    mask(virt_buf, half_weight(virt_weight), HALF // BLK)
    stores += start_all([virt_buf], [ring.at[pl.ds(ROWS, HALF)]], store, 2 * AUX)
    loads[AUX + 1].wait()
    mask(occ_buf, half_weight(occ_weight), HALF // BLK)
    stores += start_all([occ_buf], [plane.at[pl.ds(PAIR * ROWS, HALF)]], store, 2 * AUX + 1)
    for copy in stores:
        copy.wait()


def mask_inputs(mask_int, mask_occ, mask_virt, integrals, occ, virt):
    outs = (
        jax.ShapeDtypeStruct((STRIDE, COLS), BF16),
        jax.ShapeDtypeStruct((STRIDE, COLS), BF16),
        jax.ShapeDtypeStruct((AUX, ROWS, COLS), BF16),
    )
    masks = (mask_int.transpose(0, 2, 1), mask_occ.T, mask_virt.T)
    return pl.pallas_call(
        mask_kernel,
        out_shape=outs,
        in_specs=[HBM] * 6,
        out_specs=(HBM,) * 3,
        scratch_shapes=[pltpu.VMEM((AUX, ROWS, COLS), BF16)]
        + [pltpu.VMEM((HALF, COLS), BF16)] * 2
        + [pltpu.VMEM(a.shape, a.dtype) for a in masks]
        + [pltpu.SemaphoreType.DMA((5 + AUX,)), pltpu.SemaphoreType.DMA((2 + 2 * AUX,))],
        compiler_params=PARAMS,
        name="mask_inputs",
    )(*masks, integrals, occ, virt)


def tile_index(offsets):
    col, core = lax.axis_index("col"), lax.axis_index("layer")
    y, x = lax.div(col, 4), lax.rem(col, 4)
    first, second = offsets
    tile_x = lax.rem(x + jnp.where(core == 0, first, second) + 4, 4)
    tile_y = lax.rem(y + jnp.where(core == 0, second, first) + 4, 4)
    return tile_y * 4 + tile_x


def call(kernel, name, operands, outs, scratch, sems, flops):
    return pl.pallas_call(
        kernel,
        out_shape=outs,
        in_specs=[HBM] * len(operands),
        out_specs=jax.tree.map(lambda _: HBM, outs),
        scratch_shapes=scratch + [pltpu.SemaphoreType.DMA((sems,))],
        compiler_params=PARAMS,
        cost_estimate=pl.CostEstimate(flops=flops, bytes_accessed=9 << 20, transcendentals=0),
        name=name,
    )(*operands)


SUM = (PAIR * ROWS, COLS)
TILE = (HALF, COLS)


def occ_kernel(*refs):
    n = len(PLANE)
    pieces, out, buf, sems = refs[:n], refs[n], refs[n + 1], refs[n + 2]
    loads, stores = [], []
    for a, tiles in enumerate(PLANE):
        for k, offsets in enumerate(tiles):
            i = 2 * a + k
            source = pieces[a].at[pl.ds(k * STRIDE + PAIR * ROWS, HALF)]
            to = out.at[pl.ds(pl.multiple_of(tile_index(offsets) * HALF, HALF), HALF)]
            loads.append(pltpu.make_async_copy(source, buf.at[i], sems.at[i]))
            stores.append(pltpu.make_async_copy(buf.at[i], to, sems.at[2 * n + i]))
    for load in loads:
        load.start()
    for load, store in zip(loads, stores):
        load.wait()
        store.start()
    for store in stores:
        store.wait()


def occ_tiles(pieces):
    return call(
        occ_kernel, "occ_tiles", pieces, jax.ShapeDtypeStruct((16 * HALF, COLS), BF16),
        [pltpu.VMEM((16, *TILE), BF16)], 32, 0,
    )


def start_plane(arrays, rows, gathered, pieces, bufs, virt_buf, sems, first):
    copies, virt_copies = [], []
    for k, a in enumerate(arrays):
        for i, offsets in enumerate(PLANE[a]):
            sem = first + 4 * k + 2 * i
            source = pieces[k].at[pl.ds(i * rows, PAIR * ROWS)]
            copies += start_all([source], [bufs.at[2 * k + i]], sems, sem)
            start = pl.multiple_of(tile_index(offsets) * STRIDE + ROWS, HALF)
            virt_copies += start_all([gathered.at[pl.ds(start, HALF)]], [virt_buf.at[2 * k + i]], sems, sem + 1)
    return copies, virt_copies


def plane_add(copies, bufs, virt_copies, virt, acc, fresh):
    for k in range(0, len(copies), 2):
        for copy in copies[k:k + 2] + virt_copies[k:k + 2]:
            copy.wait()
        for p in range(PAIR):
            at = pl.ds(p * ROWS, ROWS)
            part = jnp.dot(bufs[k, at, :], virt[k], preferred_element_type=F32)
            part += jnp.dot(bufs[k + 1, at, :], virt[k + 1], preferred_element_type=F32)
            acc[at, :] = part if fresh and k == 0 else acc[at, :] + part


def plane_kernel(arrays, rows, gathered, *refs):
    n = len(arrays)
    pieces, out, (bufs, virt_buf, acc, out_buf, sems) = refs[:n], refs[n], refs[n + 1:]
    copies, virt_copies = start_plane(arrays, rows, gathered, pieces, bufs, virt_buf, sems, 0)
    plane_add(copies, bufs, virt_copies, virt_buf, acc, True)
    out_buf[...] = acc[...].astype(out_buf.dtype)
    pltpu.sync_copy(out_buf, out)


def plane_product(name, arrays, rows, gathered, pieces, dtype):
    n = len(arrays)
    scratch = [pltpu.VMEM((2 * n, *SUM), BF16), pltpu.VMEM((2 * n, *TILE), BF16), pltpu.VMEM(SUM, F32), pltpu.VMEM(SUM, dtype)]
    return call(
        functools.partial(plane_kernel, arrays, rows), name, (gathered, *pieces),
        jax.ShapeDtypeStruct(SUM, dtype), scratch, 4 * n, 2 << 30,
    )


def ring_kernel(stride, gap, per_chip, own, other, gathered, out, piece_buf, occ_buf, acc, out_buf, sems):
    core = lax.axis_index("layer")
    own_rows = pl.ds(pl.multiple_of(core * HALF, HALF), HALF)
    other_rows = pl.ds(pl.multiple_of((1 - core) * HALF, HALF), HALF)
    copies = []
    for z in range(8):
        group = []
        for i in range(2):
            tile = pl.ds((2 * z + i) * HALF, HALF)
            k = 2 * z + i
            group += start_all(
                [own.at[tile], other.at[tile]], [occ_buf.at[k, own_rows], occ_buf.at[k, other_rows]], sems, 6 * z + 2 * i
            )
        block = (2 * z + core if per_chip else z) * stride
        for p in range(PAIR):
            start = pl.multiple_of(block + p * (ROWS + gap), HALF)
            group += start_all([gathered.at[pl.ds(start, ROWS)]], [piece_buf.at[z, p]], sems, 6 * z + 4 + p)
        copies.append(group)
    for z in range(8):
        for copy in copies[z]:
            copy.wait()
        for p in range(PAIR):
            part = jnp.dot(occ_buf[2 * z], piece_buf[z, p, pl.ds(0, HALF), :], preferred_element_type=F32)
            part += jnp.dot(occ_buf[2 * z + 1], piece_buf[z, p, pl.ds(HALF, HALF), :], preferred_element_type=F32)
            at = pl.ds(p * ROWS, ROWS)
            acc[at, :] = part if z == 0 else acc[at, :] + part
    out_buf[...] = acc[...].astype(BF16)
    pltpu.sync_copy(out_buf, out)


def ring_product(name, own, other, gathered, stride, gap, per_chip):
    scratch = [
        pltpu.VMEM((8, PAIR, ROWS, COLS), BF16), pltpu.VMEM((16, ROWS, COLS), BF16),
        pltpu.VMEM(SUM, F32), pltpu.VMEM(SUM, BF16),
    ]
    return call(
        functools.partial(ring_kernel, stride, gap, per_chip), name, (own, other, gathered),
        jax.ShapeDtypeStruct(SUM, BF16), scratch, 48, 2 << 30,
    )


CHUNK = 32


def chi_tile(polar, aux):
    count = aux.shape[0]

    def add_rows(i, total):
        at = pl.ds(pl.multiple_of(i * CHUNK, CHUNK), CHUNK)
        left = [polar[pl.ds(pl.multiple_of(p * ROWS + i * CHUNK, CHUNK), CHUNK), :] for p in range(AUX)]
        left = jnp.concatenate(left, axis=0)
        right = jnp.concatenate([aux[q, at, :] for q in range(count)], axis=0)
        return total + lax.dot_general(left, right, (((1,), (1,)), ((), ())), preferred_element_type=F32)

    shape = (AUX * CHUNK, count * CHUNK)
    total = lax.fori_loop(0, ROWS // CHUNK, add_rows, jnp.zeros(shape, F32), unroll=4)
    rows = lax.broadcasted_iota(jnp.int32, shape, 0)
    cols = lax.broadcasted_iota(jnp.int32, shape, 1)
    total = jnp.where(lax.rem(rows, CHUNK) == lax.rem(cols, CHUNK), total, 0.0)
    sums = [jnp.sum(total[p * CHUNK:(p + 1) * CHUNK], axis=0, keepdims=True) for p in range(AUX)]
    sums = jnp.concatenate(sums + [jnp.zeros((8 - AUX, shape[1]), F32)], axis=0)
    group = lax.broadcasted_iota(jnp.int32, sums.shape, 1) // CHUNK
    rows = lax.broadcasted_iota(jnp.int32, (8, BLK), 0)
    cols = lax.broadcasted_iota(jnp.int32, (8, BLK), 1)
    result = jnp.zeros((8, BLK), F32)
    for q in range(count):
        value = jnp.sum(jnp.where(group == q, sums, 0.0), axis=1, keepdims=True)
        result = jnp.where(cols == rows * count + q, value, result)
    return jnp.sum(result, axis=0, keepdims=True)


def polar_kernel(gathered, top, bottom, plane_sum, ring_part, own_aux, other_aux, polar, chi,
                 bufs, virt_buf, acc, aux_buf, polar_buf, chi_buf, sems):
    core = lax.axis_index("layer")
    own, other = pl.ds(core * AUX, AUX), pl.ds((1 - core) * AUX, AUX)
    sum_copy, = start_all((plane_sum,), (acc,), sems)
    copies, virt_copies = start_plane((6, 7), PAIR * ROWS, gathered, (top, bottom), bufs, virt_buf, sems, 4)
    part_copies = start_all(
        (ring_part, own_aux, other_aux),
        (polar_buf.at[pl.ds(0, PAIR * ROWS)], aux_buf.at[own], aux_buf.at[other]), sems, 1
    )
    sum_copy.wait()
    plane_add(copies, bufs, virt_copies, virt_buf, acc, False)
    polar_buf[pl.ds(PAIR * ROWS, PAIR * ROWS), :] = acc[...].astype(BF16)
    for copy in part_copies:
        copy.wait()
    polar_copy, = start_all((polar_buf,), (polar,), sems)
    chi_buf[...] = jnp.broadcast_to(chi_tile(polar_buf, aux_buf), chi_buf.shape)
    pltpu.sync_copy(chi_buf, chi)
    polar_copy.wait()


def polar_product(gathered, pieces, plane_sum, ring_part, own_aux, other_aux):
    outs = (jax.ShapeDtypeStruct((AUX * ROWS, COLS), BF16), jax.ShapeDtypeStruct((128, BLK), F32))
    scratch = [pltpu.VMEM((4, *SUM), BF16), pltpu.VMEM((4, *TILE), BF16), pltpu.VMEM(SUM, F32)]
    scratch += [pltpu.VMEM((2 * AUX, ROWS, COLS), BF16)] + buffers_of(outs)
    operands = (gathered, *pieces, plane_sum, ring_part, own_aux, other_aux)
    return call(polar_kernel, "polar_product", operands, outs, scratch, 12, 1 << 29)


def body(integrals, density_occ, density_virt, mask_int, mask_occ, mask_virt):
    plane_aux, ring_aux, own_aux = mask_inputs(
        mask_int, mask_occ, mask_virt, integrals, density_occ, density_virt
    )
    gathered = lax.all_gather(ring_aux, ("row", "layer"), axis=0, tiled=True)
    plane = gather_plane(plane_aux)
    own_occ = occ_tiles(plane)
    other_occ = swap_cores(own_occ)
    half_tensor = plane_product("half_tensor", tuple(range(8)), STRIDE, gathered, plane, BF16)
    own_occ, other_occ, half_tensor = lax.optimization_barrier((own_occ, other_occ, half_tensor))
    occ_first = ring_product("occ_first", own_occ, other_occ, gathered, STRIDE, HALF, True)

    ring = lax.all_gather(half_tensor, "row", axis=0, tiled=True)
    own_aux, occ_first = lax.optimization_barrier((own_aux, occ_first))
    other_aux = swap_cores(own_aux)
    plane = gather_plane(occ_first)
    plane_sum = plane_product("plane_near", tuple(range(6)), PAIR * ROWS, gathered, plane[:6], F32)
    ring_part = ring_product("polar_ring", own_occ, other_occ, ring, PAIR * ROWS, 0, False)
    polar, chi = polar_product(gathered, plane[6:], plane_sum, ring_part, own_aux, other_aux)

    shares = lax.all_to_all(chi.reshape(128, 1, BLK), ("row", "col"), 0, 0)
    chi = jnp.sum(shares.reshape(128, BLK), axis=0) * (1.0 / (ROWS * lax.axis_size("row")))
    return polar.reshape(AUX, ROWS, COLS), chi[:2 * AUX * AUX].reshape(AUX, 2 * AUX)


def solution(mesh):
    in_specs = (
        P("layer", "row", "col"),
        P("row", "col"),
        P("row", "col"),
        P("layer", "row", "col"),
        P("row", "col"),
        P("row", "col"),
    )
    out_specs = (P("layer", "row", "col"), P("layer", None))
    return jax.shard_map(body, mesh=mesh, in_specs=in_specs, out_specs=out_specs, check_vma=False)
```

```python
import functools

import jax
import jax.numpy as jnp
from jax import lax
from jax.experimental import pallas as pl
from jax.experimental.pallas import tpu as pltpu
from jax.sharding import PartitionSpec as P

BLK = 128
ROWS = 512
COLS = 256
HALF = 256
PAIR = 2
AUX = 2 * PAIR
STRIDE = PAIR * ROWS + HALF
F32 = jnp.float32
BF16 = jnp.bfloat16
HBM = pl.BlockSpec(memory_space=pltpu.HBM)
PARAMS = pltpu.CompilerParams(vmem_limit_bytes=60 * 1024 * 1024)


def plane_index(y, x, core):
    return ((y % 4) * 4 + x % 4) * 2 + core


def plane_perm(shift, first):
    pairs = []
    for y in range(4):
        for x in range(4):
            for core in range(2):
                along_x = (core == 0) == first
                to = (y, x + shift) if along_x else (y + shift, x)
                pairs.append((plane_index(y, x, core), plane_index(*to, core)))
    return pairs


def plane_move(value, shift, first):
    return lax.ppermute(value, ("col", "layer"), plane_perm(shift, first))


def swap_cores(value):
    return lax.ppermute(value, "layer", [(0, 1), (1, 0)])


PLANE = (
    ((0, 0), (-1, 0)),
    ((1, 0), (2, 0)),
    ((0, -1), (-1, -1)),
    ((0, 1), (-1, 1)),
    ((1, -1), (2, -1)),
    ((1, 1), (2, 1)),
    ((0, 2), (-1, 2)),
    ((1, 2), (2, 2)),
)


def gather_plane(plane):
    rows = plane.shape[0]
    half = rows // 2
    before, behind = plane_move(plane, 1, True), plane_move(plane, -1, True)
    low, high = plane_move(before[:half], 1, True), plane_move(behind[half:], -1, True)
    top, = pack((plane, before), ((0, 0, rows, 0, 0), (1, 0, rows, 0, rows)), (2 * rows,))
    top_before, top_behind = plane_move(top, 1, False), plane_move(top, -1, False)
    bottom, = pack(
        (behind, low, high),
        ((0, 0, rows, 0, 0), (1, 0, half, 0, rows), (2, 0, half, 0, rows + half)),
        (2 * rows,),
    )
    bottom_before, bottom_behind = plane_move(bottom, 1, False), plane_move(bottom, -1, False)
    top_before, top_behind, bottom_before, bottom_behind = lax.optimization_barrier(
        (top_before, top_behind, bottom_before, bottom_behind)
    )
    top_far, bottom_far = plane_move(top_before, 1, False), plane_move(bottom_behind, -1, False)
    return top, bottom, top_before, top_behind, bottom_before, bottom_behind, top_far, bottom_far


def buffers_of(arrays):
    return [pltpu.VMEM(a.shape, a.dtype) for a in arrays]


def start_all(sources, buffers, sems, first=0):
    copies = [pltpu.make_async_copy(a, b, sems.at[first + i]) for i, (a, b) in enumerate(zip(sources, buffers))]
    for copy in copies:
        copy.start()
    return copies


def pack_kernel(moves, count, *refs):
    sources, outs, buf, sems = refs[:count], refs[count:-2], refs[-2], refs[-1]
    loads, stores, at = [], [], 0
    for k, (i, start, rows, o, to) in enumerate(moves):
        part = buf.at[pl.ds(at, rows)]
        loads.append(pltpu.make_async_copy(sources[i].at[pl.ds(start, rows)], part, sems.at[0, k]))
        stores.append(pltpu.make_async_copy(part, outs[o].at[pl.ds(to, rows)], sems.at[1, k]))
        at += rows
    for load in loads:
        load.start()
    for load, store in zip(loads, stores):
        load.wait()
        store.start()
    for store in stores:
        store.wait()


def pack(sources, moves, out_rows):
    return pl.pallas_call(
        functools.partial(pack_kernel, moves, len(sources)),
        out_shape=tuple(jax.ShapeDtypeStruct((rows, COLS), BF16) for rows in out_rows),
        in_specs=[HBM] * len(sources),
        out_specs=(HBM,) * len(out_rows),
        scratch_shapes=[
            pltpu.VMEM((sum(move[2] for move in moves), COLS), BF16),
            pltpu.SemaphoreType.DMA((2, len(moves))),
        ],
        compiler_params=PARAMS,
        cost_estimate=pl.CostEstimate(flops=0, bytes_accessed=4 << 20, transcendentals=0),
        name="pack",
    )(*sources)


def mask_kernel(mask_int, mask_occ, mask_virt, integrals, occ, virt, plane, ring, aux,
                int_buf, occ_buf, virt_buf, int_weight, occ_weight, virt_weight, load, store):
    core = lax.axis_index("layer")
    half = pl.ds(pl.multiple_of(core * HALF, HALF), HALF)
    weights = start_all((mask_int, mask_occ, mask_virt), (int_weight, occ_weight, virt_weight), load)
    loads = start_all([integrals.at[p] for p in range(AUX)], [int_buf.at[p] for p in range(AUX)], load, 3)
    loads += start_all([virt.at[half], occ.at[half]], [virt_buf, occ_buf], load, 3 + AUX)

    def mask(ref, weight, block_rows):
        for i in range(block_rows):
            for j in range(COLS // BLK):
                at = pl.ds(i * BLK, BLK), pl.ds(j * BLK, BLK)
                block = ref[at].astype(F32)
                ref[at] = (block * jnp.broadcast_to(weight(i, j).astype(F32), block.shape)).astype(BF16)

    def half_weight(ref):
        def weight(i, j):
            low, high = ref[pl.ds(j, 1), pl.ds(i, 1)], ref[pl.ds(j, 1), pl.ds(HALF // BLK + i, 1)]
            return jnp.where(core == 0, low, high)

        return weight

    for copy in weights:
        copy.wait()
    stores = []
    for p in range(AUX):
        loads[p].wait()
        mask(int_buf.at[p], lambda i, j: int_weight[p, pl.ds(j, 1), pl.ds(i, 1)], ROWS // BLK)
        if p < PAIR:
            to = plane.at[pl.ds(p * ROWS, ROWS)]
        else:
            to = ring.at[pl.ds((p - PAIR) * (ROWS + HALF), ROWS)]
        stores += start_all([int_buf.at[p], int_buf.at[p]], [to, aux.at[p]], store, 2 * p)
    loads[AUX].wait()
    mask(virt_buf, half_weight(virt_weight), HALF // BLK)
    stores += start_all([virt_buf], [ring.at[pl.ds(ROWS, HALF)]], store, 2 * AUX)
    loads[AUX + 1].wait()
    mask(occ_buf, half_weight(occ_weight), HALF // BLK)
    stores += start_all([occ_buf], [plane.at[pl.ds(PAIR * ROWS, HALF)]], store, 2 * AUX + 1)
    for copy in stores:
        copy.wait()


def mask_inputs(mask_int, mask_occ, mask_virt, integrals, occ, virt):
    outs = (
        jax.ShapeDtypeStruct((STRIDE, COLS), BF16),
        jax.ShapeDtypeStruct((STRIDE, COLS), BF16),
        jax.ShapeDtypeStruct((AUX, ROWS, COLS), BF16),
    )
    masks = (mask_int.transpose(0, 2, 1), mask_occ.T, mask_virt.T)
    return pl.pallas_call(
        mask_kernel,
        out_shape=outs,
        in_specs=[HBM] * 6,
        out_specs=(HBM,) * 3,
        scratch_shapes=[pltpu.VMEM((AUX, ROWS, COLS), BF16)]
        + [pltpu.VMEM((HALF, COLS), BF16)] * 2
        + [pltpu.VMEM(a.shape, a.dtype) for a in masks]
        + [pltpu.SemaphoreType.DMA((5 + AUX,)), pltpu.SemaphoreType.DMA((2 + 2 * AUX,))],
        compiler_params=PARAMS,
        name="mask_inputs",
    )(*masks, integrals, occ, virt)


def tile_index(offsets):
    col, core = lax.axis_index("col"), lax.axis_index("layer")
    y, x = lax.div(col, 4), lax.rem(col, 4)
    first, second = offsets
    tile_x = lax.rem(x + jnp.where(core == 0, first, second) + 4, 4)
    tile_y = lax.rem(y + jnp.where(core == 0, second, first) + 4, 4)
    return tile_y * 4 + tile_x


def call(kernel, name, operands, outs, scratch, sems, flops):
    return pl.pallas_call(
        kernel,
        out_shape=outs,
        in_specs=[HBM] * len(operands),
        out_specs=jax.tree.map(lambda _: HBM, outs),
        scratch_shapes=scratch + [pltpu.SemaphoreType.DMA((sems,))],
        compiler_params=PARAMS,
        cost_estimate=pl.CostEstimate(flops=flops, bytes_accessed=9 << 20, transcendentals=0),
        name=name,
    )(*operands)


SUM = (PAIR * ROWS, COLS)
TILE = (HALF, COLS)


def occ_kernel(*refs):
    n = len(PLANE)
    pieces, out, buf, sems = refs[:n], refs[n], refs[n + 1], refs[n + 2]
    loads, stores = [], []
    for a, tiles in enumerate(PLANE):
        for k, offsets in enumerate(tiles):
            i = 2 * a + k
            source = pieces[a].at[pl.ds(k * STRIDE + PAIR * ROWS, HALF)]
            to = out.at[pl.ds(pl.multiple_of(tile_index(offsets) * HALF, HALF), HALF)]
            loads.append(pltpu.make_async_copy(source, buf.at[i], sems.at[i]))
            stores.append(pltpu.make_async_copy(buf.at[i], to, sems.at[2 * n + i]))
    for load in loads:
        load.start()
    for load, store in zip(loads, stores):
        load.wait()
        store.start()
    for store in stores:
        store.wait()


def occ_tiles(pieces):
    return call(
        occ_kernel, "occ_tiles", pieces, jax.ShapeDtypeStruct((16 * HALF, COLS), BF16),
        [pltpu.VMEM((16, *TILE), BF16)], 32, 0,
    )


def start_plane(arrays, rows, gathered, pieces, bufs, virt_buf, sems, first):
    copies, virt_copies = [], []
    for k, a in enumerate(arrays):
        for i, offsets in enumerate(PLANE[a]):
            sem = first + 4 * k + 2 * i
            source = pieces[k].at[pl.ds(i * rows, PAIR * ROWS)]
            copies += start_all([source], [bufs.at[2 * k + i]], sems, sem)
            start = pl.multiple_of(tile_index(offsets) * STRIDE + ROWS, HALF)
            virt_copies += start_all([gathered.at[pl.ds(start, HALF)]], [virt_buf.at[2 * k + i]], sems, sem + 1)
    return copies, virt_copies


def plane_add(copies, bufs, virt_copies, virt, acc, fresh):
    for k in range(0, len(copies), 2):
        for copy in copies[k:k + 2] + virt_copies[k:k + 2]:
            copy.wait()
        for p in range(PAIR):
            at = pl.ds(p * ROWS, ROWS)
            part = jnp.dot(bufs[k, at, :], virt[k], preferred_element_type=F32)
            part += jnp.dot(bufs[k + 1, at, :], virt[k + 1], preferred_element_type=F32)
            acc[at, :] = part if fresh and k == 0 else acc[at, :] + part


def plane_kernel(arrays, rows, gathered, *refs):
    n = len(arrays)
    pieces, out, (bufs, virt_buf, acc, out_buf, sems) = refs[:n], refs[n], refs[n + 1:]
    copies, virt_copies = start_plane(arrays, rows, gathered, pieces, bufs, virt_buf, sems, 0)
    plane_add(copies, bufs, virt_copies, virt_buf, acc, True)
    out_buf[...] = acc[...].astype(out_buf.dtype)
    pltpu.sync_copy(out_buf, out)


def plane_product(name, arrays, rows, gathered, pieces, dtype):
    n = len(arrays)
    scratch = [pltpu.VMEM((2 * n, *SUM), BF16), pltpu.VMEM((2 * n, *TILE), BF16), pltpu.VMEM(SUM, F32), pltpu.VMEM(SUM, dtype)]
    return call(
        functools.partial(plane_kernel, arrays, rows), name, (gathered, *pieces),
        jax.ShapeDtypeStruct(SUM, dtype), scratch, 4 * n, 2 << 30,
    )


def plane_last_kernel(rows, gathered, top, bottom, sum_in, out, bufs, virt_buf, acc, out_buf, sems):
    sum_copy, = start_all([sum_in], [acc], sems)
    copies, virt_copies = start_plane((6, 7), rows, gathered, (top, bottom), bufs, virt_buf, sems, 1)
    sum_copy.wait()
    plane_add(copies, bufs, virt_copies, virt_buf, acc, False)
    out_buf[...] = acc[...].astype(BF16)
    pltpu.sync_copy(out_buf, out)


def plane_last(rows, gathered, pieces, sum_in):
    scratch = [pltpu.VMEM((4, *SUM), BF16), pltpu.VMEM((4, *TILE), BF16), pltpu.VMEM(SUM, F32), pltpu.VMEM(SUM, BF16)]
    return call(
        functools.partial(plane_last_kernel, rows), "plane_last", (gathered, *pieces, sum_in),
        jax.ShapeDtypeStruct(SUM, BF16), scratch, 9, 1 << 29,
    )


def ring_kernel(stride, gap, per_chip, own, other, gathered, out, piece_buf, occ_buf, acc, out_buf, sems):
    core = lax.axis_index("layer")
    own_rows = pl.ds(pl.multiple_of(core * HALF, HALF), HALF)
    other_rows = pl.ds(pl.multiple_of((1 - core) * HALF, HALF), HALF)
    copies = []
    for z in range(8):
        group = []
        for i in range(2):
            tile = pl.ds((2 * z + i) * HALF, HALF)
            k = 2 * z + i
            group += start_all(
                [own.at[tile], other.at[tile]], [occ_buf.at[k, own_rows], occ_buf.at[k, other_rows]], sems, 6 * z + 2 * i
            )
        block = (2 * z + core if per_chip else z) * stride
        for p in range(PAIR):
            start = pl.multiple_of(block + p * (ROWS + gap), HALF)
            group += start_all([gathered.at[pl.ds(start, ROWS)]], [piece_buf.at[z, p]], sems, 6 * z + 4 + p)
        copies.append(group)
    for z in range(8):
        for copy in copies[z]:
            copy.wait()
        for p in range(PAIR):
            part = jnp.dot(occ_buf[2 * z], piece_buf[z, p, pl.ds(0, HALF), :], preferred_element_type=F32)
            part += jnp.dot(occ_buf[2 * z + 1], piece_buf[z, p, pl.ds(HALF, HALF), :], preferred_element_type=F32)
            at = pl.ds(p * ROWS, ROWS)
            acc[at, :] = part if z == 0 else acc[at, :] + part
    out_buf[...] = acc[...].astype(BF16)
    pltpu.sync_copy(out_buf, out)


def ring_product(name, own, other, gathered, stride, gap, per_chip):
    scratch = [
        pltpu.VMEM((8, PAIR, ROWS, COLS), BF16), pltpu.VMEM((16, ROWS, COLS), BF16),
        pltpu.VMEM(SUM, F32), pltpu.VMEM(SUM, BF16),
    ]
    return call(
        functools.partial(ring_kernel, stride, gap, per_chip), name, (own, other, gathered),
        jax.ShapeDtypeStruct(SUM, BF16), scratch, 48, 2 << 30,
    )


CHUNK = 32


def chi_tile(polar, aux):
    count = aux.shape[0]

    def add_rows(i, total):
        at = pl.ds(pl.multiple_of(i * CHUNK, CHUNK), CHUNK)
        left = [polar[pl.ds(pl.multiple_of(p * ROWS + i * CHUNK, CHUNK), CHUNK), :] for p in range(AUX)]
        left = jnp.concatenate(left, axis=0)
        right = jnp.concatenate([aux[q, at, :] for q in range(count)], axis=0)
        return total + lax.dot_general(left, right, (((1,), (1,)), ((), ())), preferred_element_type=F32)

    shape = (AUX * CHUNK, count * CHUNK)
    total = lax.fori_loop(0, ROWS // CHUNK, add_rows, jnp.zeros(shape, F32), unroll=4)
    rows = lax.broadcasted_iota(jnp.int32, shape, 0)
    cols = lax.broadcasted_iota(jnp.int32, shape, 1)
    total = jnp.where(lax.rem(rows, CHUNK) == lax.rem(cols, CHUNK), total, 0.0)
    sums = [jnp.sum(total[p * CHUNK:(p + 1) * CHUNK], axis=0, keepdims=True) for p in range(AUX)]
    sums = jnp.concatenate(sums + [jnp.zeros((8 - AUX, shape[1]), F32)], axis=0)
    group = lax.broadcasted_iota(jnp.int32, sums.shape, 1) // CHUNK
    rows = lax.broadcasted_iota(jnp.int32, (8, BLK), 0)
    cols = lax.broadcasted_iota(jnp.int32, (8, BLK), 1)
    result = jnp.zeros((8, BLK), F32)
    for q in range(count):
        value = jnp.sum(jnp.where(group == q, sums, 0.0), axis=1, keepdims=True)
        result = jnp.where(cols == rows * count + q, value, result)
    return jnp.sum(result, axis=0, keepdims=True)


def polar_kernel(gathered, top, bottom, plane_sum, ring_part, own_aux, other_aux, polar, chi,
                 bufs, virt_buf, acc, aux_buf, polar_buf, chi_buf, sems):
    core = lax.axis_index("layer")
    own, other = pl.ds(core * AUX, AUX), pl.ds((1 - core) * AUX, AUX)
    sum_copy, = start_all((plane_sum,), (acc,), sems)
    copies, virt_copies = start_plane((6, 7), PAIR * ROWS, gathered, (top, bottom), bufs, virt_buf, sems, 4)
    part_copies = start_all(
        (ring_part, own_aux, other_aux),
        (polar_buf.at[pl.ds(0, PAIR * ROWS)], aux_buf.at[own], aux_buf.at[other]), sems, 1
    )
    sum_copy.wait()
    plane_add(copies, bufs, virt_copies, virt_buf, acc, False)
    polar_buf[pl.ds(PAIR * ROWS, PAIR * ROWS), :] = acc[...].astype(BF16)
    for copy in part_copies:
        copy.wait()
    polar_copy, = start_all((polar_buf,), (polar,), sems)
    chi_buf[...] = jnp.broadcast_to(chi_tile(polar_buf, aux_buf), chi_buf.shape)
    pltpu.sync_copy(chi_buf, chi)
    polar_copy.wait()


def polar_product(gathered, pieces, plane_sum, ring_part, own_aux, other_aux):
    outs = (jax.ShapeDtypeStruct((AUX * ROWS, COLS), BF16), jax.ShapeDtypeStruct((128, BLK), F32))
    scratch = [pltpu.VMEM((4, *SUM), BF16), pltpu.VMEM((4, *TILE), BF16), pltpu.VMEM(SUM, F32)]
    scratch += [pltpu.VMEM((2 * AUX, ROWS, COLS), BF16)] + buffers_of(outs)
    operands = (gathered, *pieces, plane_sum, ring_part, own_aux, other_aux)
    return call(polar_kernel, "polar_product", operands, outs, scratch, 12, 1 << 29)


def body(integrals, density_occ, density_virt, mask_int, mask_occ, mask_virt):
    plane_aux, ring_aux, own_aux = mask_inputs(
        mask_int, mask_occ, mask_virt, integrals, density_occ, density_virt
    )
    gathered = lax.all_gather(ring_aux, ("row", "layer"), axis=0, tiled=True)
    plane = gather_plane(plane_aux)
    plane_sum = plane_product("plane_near", tuple(range(6)), STRIDE, gathered, plane[:6], F32)
    *far, plane_sum = lax.optimization_barrier((*plane[6:], plane_sum))
    own_occ = occ_tiles((*plane[:6], *far))
    other_occ = swap_cores(own_occ)
    half_tensor = plane_last(STRIDE, gathered, far, plane_sum)
    own_occ, other_occ, half_tensor = lax.optimization_barrier((own_occ, other_occ, half_tensor))
    occ_first = ring_product("occ_first", own_occ, other_occ, gathered, STRIDE, HALF, True)

    ring = lax.all_gather(half_tensor, "row", axis=0, tiled=True)
    own_aux, occ_first = lax.optimization_barrier((own_aux, occ_first))
    other_aux = swap_cores(own_aux)
    plane = gather_plane(occ_first)
    plane_sum = plane_product("plane_near", tuple(range(6)), PAIR * ROWS, gathered, plane[:6], F32)
    ring_part = ring_product("polar_ring", own_occ, other_occ, ring, PAIR * ROWS, 0, False)
    polar, chi = polar_product(gathered, plane[6:], plane_sum, ring_part, own_aux, other_aux)

    shares = lax.all_to_all(chi.reshape(128, 1, BLK), ("row", "col"), 0, 0)
    chi = jnp.sum(shares.reshape(128, BLK), axis=0) * (1.0 / (ROWS * lax.axis_size("row")))
    return polar.reshape(AUX, ROWS, COLS), chi[:2 * AUX * AUX].reshape(AUX, 2 * AUX)


def solution(mesh):
    in_specs = (
        P("layer", "row", "col"),
        P("row", "col"),
        P("row", "col"),
        P("layer", "row", "col"),
        P("row", "col"),
        P("row", "col"),
    )
    out_specs = (P("layer", "row", "col"), P("layer", None))
    return jax.shard_map(body, mesh=mesh, in_specs=in_specs, out_specs=out_specs, check_vma=False)
```

```python
import functools

import jax
import jax.numpy as jnp
from jax import lax
from jax.experimental import pallas as pl
from jax.experimental.pallas import tpu as pltpu
from jax.sharding import PartitionSpec as P

BLK = 128
ROWS = 512
COLS = 256
HALF = 256
PAIR = 2
AUX = 2 * PAIR
STRIDE = PAIR * ROWS + HALF
F32 = jnp.float32
BF16 = jnp.bfloat16
HBM = pl.BlockSpec(memory_space=pltpu.HBM)
ANY = pl.BlockSpec(memory_space=pl.ANY)
PARAMS = pltpu.CompilerParams(vmem_limit_bytes=60 * 1024 * 1024)


def plane_index(y, x, core):
    return ((y % 4) * 4 + x % 4) * 2 + core


def plane_perm(shift, first):
    pairs = []
    for y in range(4):
        for x in range(4):
            for core in range(2):
                along_x = (core == 0) == first
                to = (y, x + shift) if along_x else (y + shift, x)
                pairs.append((plane_index(y, x, core), plane_index(*to, core)))
    return pairs


def plane_move(value, shift, first):
    return lax.ppermute(value, ("col", "layer"), plane_perm(shift, first))


def swap_cores(value):
    return lax.ppermute(value, "layer", [(0, 1), (1, 0)])


PLANE = (
    ((0, 0), (-1, 0)),
    ((1, 0), (2, 0)),
    ((0, -1), (-1, -1)),
    ((0, 1), (-1, 1)),
    ((1, -1), (2, -1)),
    ((1, 1), (2, 1)),
    ((0, 2), (-1, 2)),
    ((1, 2), (2, 2)),
)


def gather_plane(plane):
    rows = plane.shape[0]
    half = rows // 2
    before, behind = plane_move(plane, 1, True), plane_move(plane, -1, True)
    low, high = plane_move(before[:half], 1, True), plane_move(behind[half:], -1, True)
    top, = pack((plane, before), ((0, 0, rows, 0, 0), (1, 0, rows, 0, rows)), (2 * rows,))
    top_before, top_behind = plane_move(top, 1, False), plane_move(top, -1, False)
    bottom, = pack(
        (behind, low, high),
        ((0, 0, rows, 0, 0), (1, 0, half, 0, rows), (2, 0, half, 0, rows + half)),
        (2 * rows,),
    )
    bottom_before, bottom_behind = plane_move(bottom, 1, False), plane_move(bottom, -1, False)
    top_before, top_behind, bottom_before, bottom_behind = lax.optimization_barrier(
        (top_before, top_behind, bottom_before, bottom_behind)
    )
    top_far, bottom_far = plane_move(top_before, 1, False), plane_move(bottom_behind, -1, False)
    return top, bottom, top_before, top_behind, bottom_before, bottom_behind, top_far, bottom_far


def buffers_of(arrays):
    return [pltpu.VMEM(a.shape, a.dtype) for a in arrays]


def start_all(sources, buffers, sems, first=0):
    copies = [pltpu.make_async_copy(a, b, sems.at[first + i]) for i, (a, b) in enumerate(zip(sources, buffers))]
    for copy in copies:
        copy.start()
    return copies


def pack_kernel(moves, count, *refs):
    sources, outs, buf, sems = refs[:count], refs[count:-2], refs[-2], refs[-1]
    loads, stores, at = [], [], 0
    for k, (i, start, rows, o, to) in enumerate(moves):
        part = buf.at[pl.ds(at, rows)]
        loads.append(pltpu.make_async_copy(sources[i].at[pl.ds(start, rows)], part, sems.at[0, k]))
        stores.append(pltpu.make_async_copy(part, outs[o].at[pl.ds(to, rows)], sems.at[1, k]))
        at += rows
    for load in loads:
        load.start()
    for load, store in zip(loads, stores):
        load.wait()
        store.start()
    for store in stores:
        store.wait()


def pack(sources, moves, out_rows):
    return pl.pallas_call(
        functools.partial(pack_kernel, moves, len(sources)),
        out_shape=tuple(jax.ShapeDtypeStruct((rows, COLS), BF16) for rows in out_rows),
        in_specs=[ANY] * len(sources),
        out_specs=(HBM,) * len(out_rows),
        scratch_shapes=[
            pltpu.VMEM((sum(move[2] for move in moves), COLS), BF16),
            pltpu.SemaphoreType.DMA((2, len(moves))),
        ],
        compiler_params=pltpu.CompilerParams(vmem_limit_bytes=8 * 1024 * 1024),
        cost_estimate=pl.CostEstimate(flops=0, bytes_accessed=4 << 20, transcendentals=0),
        name="pack",
    )(*sources)


def mask_kernel(mask_int, mask_occ, mask_virt, integrals, occ, virt, plane, ring, aux,
                int_buf, occ_buf, virt_buf, int_weight, occ_weight, virt_weight, load, store):
    core = lax.axis_index("layer")
    half = pl.ds(pl.multiple_of(core * HALF, HALF), HALF)
    weights = start_all((mask_int, mask_occ, mask_virt), (int_weight, occ_weight, virt_weight), load)
    loads = start_all([integrals.at[p] for p in range(AUX)], [int_buf.at[p] for p in range(AUX)], load, 3)
    loads += start_all([virt.at[half], occ.at[half]], [virt_buf, occ_buf], load, 3 + AUX)

    def mask(ref, weight, block_rows):
        for i in range(block_rows):
            for j in range(COLS // BLK):
                at = pl.ds(i * BLK, BLK), pl.ds(j * BLK, BLK)
                block = ref[at].astype(F32)
                ref[at] = (block * jnp.broadcast_to(weight(i, j).astype(F32), block.shape)).astype(BF16)

    def half_weight(ref):
        def weight(i, j):
            low, high = ref[pl.ds(j, 1), pl.ds(i, 1)], ref[pl.ds(j, 1), pl.ds(HALF // BLK + i, 1)]
            return jnp.where(core == 0, low, high)

        return weight

    for copy in weights:
        copy.wait()
    stores = []
    for p in range(AUX):
        loads[p].wait()
        mask(int_buf.at[p], lambda i, j: int_weight[p, pl.ds(j, 1), pl.ds(i, 1)], ROWS // BLK)
        if p < PAIR:
            to = plane.at[pl.ds(p * ROWS, ROWS)]
        else:
            to = ring.at[pl.ds((p - PAIR) * (ROWS + HALF), ROWS)]
        stores += start_all([int_buf.at[p], int_buf.at[p]], [to, aux.at[p]], store, 2 * p)
    loads[AUX].wait()
    mask(virt_buf, half_weight(virt_weight), HALF // BLK)
    stores += start_all([virt_buf], [ring.at[pl.ds(ROWS, HALF)]], store, 2 * AUX)
    loads[AUX + 1].wait()
    mask(occ_buf, half_weight(occ_weight), HALF // BLK)
    stores += start_all([occ_buf], [plane.at[pl.ds(PAIR * ROWS, HALF)]], store, 2 * AUX + 1)
    for copy in stores:
        copy.wait()


def mask_inputs(mask_int, mask_occ, mask_virt, integrals, occ, virt):
    outs = (
        jax.ShapeDtypeStruct((STRIDE, COLS), BF16),
        jax.ShapeDtypeStruct((STRIDE, COLS), BF16),
        jax.ShapeDtypeStruct((AUX, ROWS, COLS), BF16),
    )
    masks = (mask_int.transpose(0, 2, 1), mask_occ.T, mask_virt.T)
    return pl.pallas_call(
        mask_kernel,
        out_shape=outs,
        in_specs=[HBM] * 6,
        out_specs=(HBM,) * 3,
        scratch_shapes=[pltpu.VMEM((AUX, ROWS, COLS), BF16)]
        + [pltpu.VMEM((HALF, COLS), BF16)] * 2
        + [pltpu.VMEM(a.shape, a.dtype) for a in masks]
        + [pltpu.SemaphoreType.DMA((5 + AUX,)), pltpu.SemaphoreType.DMA((2 + 2 * AUX,))],
        compiler_params=PARAMS,
        name="mask_inputs",
    )(*masks, integrals, occ, virt)


def tile_index(offsets):
    col, core = lax.axis_index("col"), lax.axis_index("layer")
    y, x = lax.div(col, 4), lax.rem(col, 4)
    first, second = offsets
    tile_x = lax.rem(x + jnp.where(core == 0, first, second) + 4, 4)
    tile_y = lax.rem(y + jnp.where(core == 0, second, first) + 4, 4)
    return tile_y * 4 + tile_x


def call(kernel, name, operands, outs, scratch, sems, flops, vmem):
    return pl.pallas_call(
        kernel,
        out_shape=outs,
        in_specs=[HBM] * len(operands),
        out_specs=jax.tree.map(lambda _: HBM, outs),
        scratch_shapes=scratch + [pltpu.SemaphoreType.DMA((sems,))],
        compiler_params=pltpu.CompilerParams(vmem_limit_bytes=vmem * 1024 * 1024),
        cost_estimate=pl.CostEstimate(flops=flops, bytes_accessed=9 << 20, transcendentals=0),
        name=name,
    )(*operands)


SUM = (PAIR * ROWS, COLS)
TILE = (HALF, COLS)


def occ_kernel(*refs):
    n = len(PLANE)
    pieces, out, buf, sems = refs[:n], refs[n], refs[n + 1], refs[n + 2]
    loads, stores = [], []
    for a, tiles in enumerate(PLANE):
        for k, offsets in enumerate(tiles):
            i = 2 * a + k
            source = pieces[a].at[pl.ds(k * STRIDE + PAIR * ROWS, HALF)]
            to = out.at[pl.ds(pl.multiple_of(tile_index(offsets) * HALF, HALF), HALF)]
            loads.append(pltpu.make_async_copy(source, buf.at[i], sems.at[i]))
            stores.append(pltpu.make_async_copy(buf.at[i], to, sems.at[2 * n + i]))
    for load in loads:
        load.start()
    for load, store in zip(loads, stores):
        load.wait()
        store.start()
    for store in stores:
        store.wait()


def occ_tiles(pieces):
    return call(
        occ_kernel, "occ_tiles", pieces, jax.ShapeDtypeStruct((16 * HALF, COLS), BF16),
        [pltpu.VMEM((16, *TILE), BF16)], 32, 0, 60,
    )


def start_plane(arrays, rows, gathered, pieces, bufs, virt_buf, sems, first):
    copies, virt_copies = [], []
    for k, a in enumerate(arrays):
        for i, offsets in enumerate(PLANE[a]):
            sem = first + 4 * k + 2 * i
            source = pieces[k].at[pl.ds(i * rows, PAIR * ROWS)]
            copies += start_all([source], [bufs.at[2 * k + i]], sems, sem)
            start = pl.multiple_of(tile_index(offsets) * STRIDE + ROWS, HALF)
            virt_copies += start_all([gathered.at[pl.ds(start, HALF)]], [virt_buf.at[2 * k + i]], sems, sem + 1)
    return copies, virt_copies


def plane_add(copies, bufs, virt_copies, virt, acc, fresh):
    for k in range(0, len(copies), 2):
        for copy in copies[k:k + 2] + virt_copies[k:k + 2]:
            copy.wait()
        for p in range(PAIR):
            at = pl.ds(p * ROWS, ROWS)
            part = jnp.dot(bufs[k, at, :], virt[k], preferred_element_type=F32)
            part += jnp.dot(bufs[k + 1, at, :], virt[k + 1], preferred_element_type=F32)
            acc[at, :] = part if fresh and k == 0 else acc[at, :] + part


def plane_kernel(arrays, rows, gathered, *refs):
    n = len(arrays)
    pieces, out, (bufs, virt_buf, acc, out_buf, sems) = refs[:n], refs[n], refs[n + 1:]
    copies, virt_copies = start_plane(arrays, rows, gathered, pieces, bufs, virt_buf, sems, 0)
    plane_add(copies, bufs, virt_copies, virt_buf, acc, True)
    out_buf[...] = acc[...].astype(out_buf.dtype)
    pltpu.sync_copy(out_buf, out)


def plane_product(name, arrays, rows, gathered, pieces, dtype):
    n = len(arrays)
    scratch = [pltpu.VMEM((2 * n, *SUM), BF16), pltpu.VMEM((2 * n, *TILE), BF16), pltpu.VMEM(SUM, F32), pltpu.VMEM(SUM, dtype)]
    return call(
        functools.partial(plane_kernel, arrays, rows), name, (gathered, *pieces),
        jax.ShapeDtypeStruct(SUM, dtype), scratch, 4 * n, 2 << 30, 51,
    )


def plane_last_kernel(rows, gathered, top, bottom, sum_in, out, bufs, virt_buf, acc, out_buf, sems):
    sum_copy, = start_all([sum_in], [acc], sems)
    copies, virt_copies = start_plane((6, 7), rows, gathered, (top, bottom), bufs, virt_buf, sems, 1)
    sum_copy.wait()
    plane_add(copies, bufs, virt_copies, virt_buf, acc, False)
    out_buf[...] = acc[...].astype(BF16)
    pltpu.sync_copy(out_buf, out)


def plane_last(rows, gathered, pieces, sum_in):
    scratch = [pltpu.VMEM((4, *SUM), BF16), pltpu.VMEM((4, *TILE), BF16), pltpu.VMEM(SUM, F32), pltpu.VMEM(SUM, BF16)]
    return call(
        functools.partial(plane_last_kernel, rows), "plane_last", (gathered, *pieces, sum_in),
        jax.ShapeDtypeStruct(SUM, BF16), scratch, 9, 1 << 29, 60,
    )


def ring_kernel(stride, gap, per_chip, own, other, gathered, out, piece_buf, occ_buf, acc, out_buf, sems):
    core = lax.axis_index("layer")
    own_rows = pl.ds(pl.multiple_of(core * HALF, HALF), HALF)
    other_rows = pl.ds(pl.multiple_of((1 - core) * HALF, HALF), HALF)
    copies = []
    for z in range(8):
        group = []
        for i in range(2):
            tile = pl.ds((2 * z + i) * HALF, HALF)
            k = 2 * z + i
            group += start_all(
                [own.at[tile], other.at[tile]], [occ_buf.at[k, own_rows], occ_buf.at[k, other_rows]], sems, 6 * z + 2 * i
            )
        block = (2 * z + core if per_chip else z) * stride
        for p in range(PAIR):
            start = pl.multiple_of(block + p * (ROWS + gap), HALF)
            group += start_all([gathered.at[pl.ds(start, ROWS)]], [piece_buf.at[z, p]], sems, 6 * z + 4 + p)
        copies.append(group)
    for z in range(8):
        for copy in copies[z]:
            copy.wait()
        for p in range(PAIR):
            part = jnp.dot(occ_buf[2 * z], piece_buf[z, p, pl.ds(0, HALF), :], preferred_element_type=F32)
            part += jnp.dot(occ_buf[2 * z + 1], piece_buf[z, p, pl.ds(HALF, HALF), :], preferred_element_type=F32)
            at = pl.ds(p * ROWS, ROWS)
            acc[at, :] = part if z == 0 else acc[at, :] + part
    out_buf[...] = acc[...].astype(BF16)
    pltpu.sync_copy(out_buf, out)


def ring_product(name, own, other, gathered, stride, gap, per_chip):
    scratch = [
        pltpu.VMEM((8, PAIR, ROWS, COLS), BF16), pltpu.VMEM((16, ROWS, COLS), BF16),
        pltpu.VMEM(SUM, F32), pltpu.VMEM(SUM, BF16),
    ]
    return call(
        functools.partial(ring_kernel, stride, gap, per_chip), name, (own, other, gathered),
        jax.ShapeDtypeStruct(SUM, BF16), scratch, 48, 2 << 30, 60 if per_chip else 60,
    )


CHUNK = 32


def chi_tile(polar, aux):
    count = aux.shape[0]

    def add_rows(i, total):
        at = pl.ds(pl.multiple_of(i * CHUNK, CHUNK), CHUNK)
        left = [polar[pl.ds(pl.multiple_of(p * ROWS + i * CHUNK, CHUNK), CHUNK), :] for p in range(AUX)]
        left = jnp.concatenate(left, axis=0)
        right = jnp.concatenate([aux[q, at, :] for q in range(count)], axis=0)
        return total + lax.dot_general(left, right, (((1,), (1,)), ((), ())), preferred_element_type=F32)

    shape = (AUX * CHUNK, count * CHUNK)
    total = lax.fori_loop(0, ROWS // CHUNK, add_rows, jnp.zeros(shape, F32), unroll=4)
    rows = lax.broadcasted_iota(jnp.int32, shape, 0)
    cols = lax.broadcasted_iota(jnp.int32, shape, 1)
    total = jnp.where(lax.rem(rows, CHUNK) == lax.rem(cols, CHUNK), total, 0.0)
    sums = [jnp.sum(total[p * CHUNK:(p + 1) * CHUNK], axis=0, keepdims=True) for p in range(AUX)]
    sums = jnp.concatenate(sums + [jnp.zeros((8 - AUX, shape[1]), F32)], axis=0)
    group = lax.broadcasted_iota(jnp.int32, sums.shape, 1) // CHUNK
    rows = lax.broadcasted_iota(jnp.int32, (8, BLK), 0)
    cols = lax.broadcasted_iota(jnp.int32, (8, BLK), 1)
    result = jnp.zeros((8, BLK), F32)
    for q in range(count):
        value = jnp.sum(jnp.where(group == q, sums, 0.0), axis=1, keepdims=True)
        result = jnp.where(cols == rows * count + q, value, result)
    return jnp.sum(result, axis=0, keepdims=True)


def polar_kernel(gathered, top, bottom, plane_sum, ring_part, own_aux, other_aux, polar, chi,
                 bufs, virt_buf, acc, aux_buf, polar_buf, chi_buf, sems):
    core = lax.axis_index("layer")
    own, other = pl.ds(core * AUX, AUX), pl.ds((1 - core) * AUX, AUX)
    sum_copy, = start_all((plane_sum,), (acc,), sems)
    copies, virt_copies = start_plane((6, 7), PAIR * ROWS, gathered, (top, bottom), bufs, virt_buf, sems, 4)
    part_copies = start_all(
        (ring_part, own_aux, other_aux),
        (polar_buf.at[pl.ds(0, PAIR * ROWS)], aux_buf.at[own], aux_buf.at[other]), sems, 1
    )
    sum_copy.wait()
    plane_add(copies, bufs, virt_copies, virt_buf, acc, False)
    polar_buf[pl.ds(PAIR * ROWS, PAIR * ROWS), :] = acc[...].astype(BF16)
    for copy in part_copies:
        copy.wait()
    polar_copy, = start_all((polar_buf,), (polar,), sems)
    chi_buf[...] = jnp.broadcast_to(chi_tile(polar_buf, aux_buf), chi_buf.shape)
    pltpu.sync_copy(chi_buf, chi)
    polar_copy.wait()


def polar_product(gathered, pieces, plane_sum, ring_part, own_aux, other_aux):
    outs = (jax.ShapeDtypeStruct((AUX * ROWS, COLS), BF16), jax.ShapeDtypeStruct((128, BLK), F32))
    scratch = [pltpu.VMEM((4, *SUM), BF16), pltpu.VMEM((4, *TILE), BF16), pltpu.VMEM(SUM, F32)]
    scratch += [pltpu.VMEM((2 * AUX, ROWS, COLS), BF16)] + buffers_of(outs)
    operands = (gathered, *pieces, plane_sum, ring_part, own_aux, other_aux)
    return call(polar_kernel, "polar_product", operands, outs, scratch, 12, 1 << 29, 60)


def body(integrals, density_occ, density_virt, mask_int, mask_occ, mask_virt):
    plane_aux, ring_aux, own_aux = mask_inputs(
        mask_int, mask_occ, mask_virt, integrals, density_occ, density_virt
    )
    gathered = lax.all_gather(ring_aux, ("row", "layer"), axis=0, tiled=True)
    plane = gather_plane(plane_aux)
    plane_sum = plane_product("plane_near", tuple(range(6)), STRIDE, gathered, plane[:6], F32)
    *far, plane_sum = lax.optimization_barrier((*plane[6:], plane_sum))
    own_occ = occ_tiles((*plane[:6], *far))
    other_occ = swap_cores(own_occ)
    half_tensor = plane_last(STRIDE, gathered, far, plane_sum)
    own_occ, other_occ, half_tensor = lax.optimization_barrier((own_occ, other_occ, half_tensor))
    occ_first = ring_product("occ_first", own_occ, other_occ, gathered, STRIDE, HALF, True)

    ring = lax.all_gather(half_tensor, "row", axis=0, tiled=True)
    own_aux, occ_first = lax.optimization_barrier((own_aux, occ_first))
    other_aux = swap_cores(own_aux)
    plane = gather_plane(occ_first)
    plane_sum = plane_product("plane_near", tuple(range(6)), PAIR * ROWS, gathered, plane[:6], F32)
    ring_part = ring_product("polar_ring", own_occ, other_occ, ring, PAIR * ROWS, 0, False)
    polar, chi = polar_product(gathered, plane[6:], plane_sum, ring_part, own_aux, other_aux)

    shares = lax.all_to_all(chi.reshape(128, 1, BLK), ("row", "col"), 0, 0)
    chi = jnp.sum(shares.reshape(128, BLK), axis=0) * (1.0 / (ROWS * lax.axis_size("row")))
    return polar.reshape(AUX, ROWS, COLS), chi[:2 * AUX * AUX].reshape(AUX, 2 * AUX)


def solution(mesh):
    in_specs = (
        P("layer", "row", "col"),
        P("row", "col"),
        P("row", "col"),
        P("layer", "row", "col"),
        P("row", "col"),
        P("row", "col"),
    )
    out_specs = (P("layer", "row", "col"), P("layer", None))
    return jax.shard_map(body, mesh=mesh, in_specs=in_specs, out_specs=out_specs, check_vma=False)
```

```python
import functools

import jax
import jax.numpy as jnp
from jax import lax
from jax.experimental import pallas as pl
from jax.experimental.pallas import tpu as pltpu
from jax.sharding import PartitionSpec as P

BLK = 128
ROWS = 512
COLS = 256
HALF = 256
PAIR = 2
AUX = 2 * PAIR
STRIDE = PAIR * ROWS + HALF
F32 = jnp.float32
BF16 = jnp.bfloat16
HBM = pl.BlockSpec(memory_space=pltpu.HBM)
ANY = pl.BlockSpec(memory_space=pl.ANY)
PARAMS = pltpu.CompilerParams(vmem_limit_bytes=60 * 1024 * 1024)


def plane_index(y, x, core):
    return ((y % 4) * 4 + x % 4) * 2 + core


def plane_perm(shift, first):
    pairs = []
    for y in range(4):
        for x in range(4):
            for core in range(2):
                along_x = (core == 0) == first
                to = (y, x + shift) if along_x else (y + shift, x)
                pairs.append((plane_index(y, x, core), plane_index(*to, core)))
    return pairs


def plane_move(value, shift, first):
    return lax.ppermute(value, ("col", "layer"), plane_perm(shift, first))


def swap_cores(value):
    return lax.ppermute(value, "layer", [(0, 1), (1, 0)])


PLANE = (
    ((0, 0), (-1, 0)),
    ((1, 0), (2, 0)),
    ((0, -1), (-1, -1)),
    ((0, 1), (-1, 1)),
    ((1, -1), (2, -1)),
    ((1, 1), (2, 1)),
    ((0, 2), (-1, 2)),
    ((1, 2), (2, 2)),
)


def gather_plane(plane):
    rows = plane.shape[0]
    half = rows // 2
    before, behind = plane_move(plane, 1, True), plane_move(plane, -1, True)
    low, high = plane_move(before[:half], 1, True), plane_move(behind[half:], -1, True)
    top, = pack((plane, before), ((0, 0, rows, 0, 0), (1, 0, rows, 0, rows)), (2 * rows,))
    top_before, top_behind = plane_move(top, 1, False), plane_move(top, -1, False)
    bottom, = pack(
        (behind, low, high),
        ((0, 0, rows, 0, 0), (1, 0, half, 0, rows), (2, 0, half, 0, rows + half)),
        (2 * rows,),
    )
    bottom_before, bottom_behind = plane_move(bottom, 1, False), plane_move(bottom, -1, False)
    top_before, top_behind, bottom_before, bottom_behind = lax.optimization_barrier(
        (top_before, top_behind, bottom_before, bottom_behind)
    )
    top_far, bottom_far = plane_move(top_before, 1, False), plane_move(bottom_behind, -1, False)
    return top, bottom, top_before, top_behind, bottom_before, bottom_behind, top_far, bottom_far


def buffers_of(arrays):
    return [pltpu.VMEM(a.shape, a.dtype) for a in arrays]


def start_all(sources, buffers, sems, first=0):
    copies = [pltpu.make_async_copy(a, b, sems.at[first + i]) for i, (a, b) in enumerate(zip(sources, buffers))]
    for copy in copies:
        copy.start()
    return copies


def pack_kernel(moves, count, *refs):
    sources, outs, buf, sems = refs[:count], refs[count:-2], refs[-2], refs[-1]
    loads, stores, at = [], [], 0
    for k, (i, start, rows, o, to) in enumerate(moves):
        part = buf.at[pl.ds(at, rows)]
        loads.append(pltpu.make_async_copy(sources[i].at[pl.ds(start, rows)], part, sems.at[0, k]))
        stores.append(pltpu.make_async_copy(part, outs[o].at[pl.ds(to, rows)], sems.at[1, k]))
        at += rows
    for load in loads:
        load.start()
    for load, store in zip(loads, stores):
        load.wait()
        store.start()
    for store in stores:
        store.wait()


def pack(sources, moves, out_rows):
    return pl.pallas_call(
        functools.partial(pack_kernel, moves, len(sources)),
        out_shape=tuple(jax.ShapeDtypeStruct((rows, COLS), BF16) for rows in out_rows),
        in_specs=[ANY] * len(sources),
        out_specs=(HBM,) * len(out_rows),
        scratch_shapes=[
            pltpu.VMEM((sum(move[2] for move in moves), COLS), BF16),
            pltpu.SemaphoreType.DMA((2, len(moves))),
        ],
        compiler_params=pltpu.CompilerParams(vmem_limit_bytes=8 * 1024 * 1024),
        cost_estimate=pl.CostEstimate(flops=0, bytes_accessed=4 << 20, transcendentals=0),
        name="pack",
    )(*sources)


def mask_kernel(mask_int, mask_occ, mask_virt, integrals, occ, virt, plane, ring, aux,
                int_buf, occ_buf, virt_buf, int_weight, occ_weight, virt_weight, load, store):
    core = lax.axis_index("layer")
    half = pl.ds(pl.multiple_of(core * HALF, HALF), HALF)
    weights = start_all((mask_int, mask_occ, mask_virt), (int_weight, occ_weight, virt_weight), load)
    loads = start_all([integrals.at[p] for p in range(AUX)], [int_buf.at[p] for p in range(AUX)], load, 3)
    loads += start_all([virt.at[half], occ.at[half]], [virt_buf, occ_buf], load, 3 + AUX)

    def mask(ref, weight, block_rows):
        for i in range(block_rows):
            for j in range(COLS // BLK):
                at = pl.ds(i * BLK, BLK), pl.ds(j * BLK, BLK)
                block = ref[at].astype(F32)
                ref[at] = (block * jnp.broadcast_to(weight(i, j).astype(F32), block.shape)).astype(BF16)

    def half_weight(ref):
        def weight(i, j):
            low, high = ref[pl.ds(j, 1), pl.ds(i, 1)], ref[pl.ds(j, 1), pl.ds(HALF // BLK + i, 1)]
            return jnp.where(core == 0, low, high)

        return weight

    for copy in weights:
        copy.wait()
    stores = []
    for p in range(AUX):
        loads[p].wait()
        mask(int_buf.at[p], lambda i, j: int_weight[p, pl.ds(j, 1), pl.ds(i, 1)], ROWS // BLK)
        if p < PAIR:
            to = plane.at[pl.ds(p * ROWS, ROWS)]
        else:
            to = ring.at[pl.ds((p - PAIR) * (ROWS + HALF), ROWS)]
        stores += start_all([int_buf.at[p], int_buf.at[p]], [to, aux.at[p]], store, 2 * p)
    loads[AUX].wait()
    mask(virt_buf, half_weight(virt_weight), HALF // BLK)
    stores += start_all([virt_buf], [ring.at[pl.ds(ROWS, HALF)]], store, 2 * AUX)
    loads[AUX + 1].wait()
    mask(occ_buf, half_weight(occ_weight), HALF // BLK)
    stores += start_all([occ_buf], [plane.at[pl.ds(PAIR * ROWS, HALF)]], store, 2 * AUX + 1)
    for copy in stores:
        copy.wait()


def mask_inputs(mask_int, mask_occ, mask_virt, integrals, occ, virt):
    outs = (
        jax.ShapeDtypeStruct((STRIDE, COLS), BF16),
        jax.ShapeDtypeStruct((STRIDE, COLS), BF16),
        jax.ShapeDtypeStruct((AUX, ROWS, COLS), BF16),
    )
    masks = (mask_int.transpose(0, 2, 1), mask_occ.T, mask_virt.T)
    return pl.pallas_call(
        mask_kernel,
        out_shape=outs,
        in_specs=[HBM] * 6,
        out_specs=(HBM,) * 3,
        scratch_shapes=[pltpu.VMEM((AUX, ROWS, COLS), BF16)]
        + [pltpu.VMEM((HALF, COLS), BF16)] * 2
        + [pltpu.VMEM(a.shape, a.dtype) for a in masks]
        + [pltpu.SemaphoreType.DMA((5 + AUX,)), pltpu.SemaphoreType.DMA((2 + 2 * AUX,))],
        compiler_params=PARAMS,
        name="mask_inputs",
    )(*masks, integrals, occ, virt)


def tile_index(offsets):
    col, core = lax.axis_index("col"), lax.axis_index("layer")
    y, x = lax.div(col, 4), lax.rem(col, 4)
    first, second = offsets
    tile_x = lax.rem(x + jnp.where(core == 0, first, second) + 4, 4)
    tile_y = lax.rem(y + jnp.where(core == 0, second, first) + 4, 4)
    return tile_y * 4 + tile_x


def call(kernel, name, operands, outs, scratch, sems, flops, vmem):
    return pl.pallas_call(
        kernel,
        out_shape=outs,
        in_specs=[HBM] * len(operands),
        out_specs=jax.tree.map(lambda _: HBM, outs),
        scratch_shapes=scratch + [pltpu.SemaphoreType.DMA((sems,))],
        compiler_params=pltpu.CompilerParams(vmem_limit_bytes=vmem * 1024 * 1024),
        cost_estimate=pl.CostEstimate(flops=flops, bytes_accessed=9 << 20, transcendentals=0),
        name=name,
    )(*operands)


SUM = (PAIR * ROWS, COLS)
TILE = (HALF, COLS)


def occ_kernel(*refs):
    n = len(PLANE)
    pieces, out, buf, sems = refs[:n], refs[n], refs[n + 1], refs[n + 2]
    loads, stores = [], []
    for a, tiles in enumerate(PLANE):
        for k, offsets in enumerate(tiles):
            i = 2 * a + k
            source = pieces[a].at[pl.ds(k * STRIDE + PAIR * ROWS, HALF)]
            to = out.at[pl.ds(pl.multiple_of(tile_index(offsets) * HALF, HALF), HALF)]
            loads.append(pltpu.make_async_copy(source, buf.at[i], sems.at[i]))
            stores.append(pltpu.make_async_copy(buf.at[i], to, sems.at[2 * n + i]))
    for load in loads:
        load.start()
    for load, store in zip(loads, stores):
        load.wait()
        store.start()
    for store in stores:
        store.wait()


def occ_tiles(pieces):
    return call(
        occ_kernel, "occ_tiles", pieces, jax.ShapeDtypeStruct((16 * HALF, COLS), BF16),
        [pltpu.VMEM((16, *TILE), BF16)], 32, 0, 60,
    )


def start_plane(arrays, rows, gathered, pieces, bufs, virt_buf, sems, first):
    copies, virt_copies = [], []
    for k, a in enumerate(arrays):
        for i, offsets in enumerate(PLANE[a]):
            sem = first + 4 * k + 2 * i
            source = pieces[k].at[pl.ds(i * rows, PAIR * ROWS)]
            copies += start_all([source], [bufs.at[2 * k + i]], sems, sem)
            start = pl.multiple_of(tile_index(offsets) * STRIDE + ROWS, HALF)
            virt_copies += start_all([gathered.at[pl.ds(start, HALF)]], [virt_buf.at[2 * k + i]], sems, sem + 1)
    return copies, virt_copies


def plane_add(copies, bufs, virt_copies, virt, acc, fresh):
    for k in range(0, len(copies), 2):
        for copy in copies[k:k + 2] + virt_copies[k:k + 2]:
            copy.wait()
        for p in range(PAIR):
            at = pl.ds(p * ROWS, ROWS)
            part = jnp.dot(bufs[k, at, :], virt[k], preferred_element_type=F32)
            part += jnp.dot(bufs[k + 1, at, :], virt[k + 1], preferred_element_type=F32)
            acc[at, :] = part if fresh and k == 0 else acc[at, :] + part


def plane_kernel(arrays, rows, gathered, *refs):
    n = len(arrays)
    pieces, out, (bufs, virt_buf, acc, out_buf, sems) = refs[:n], refs[n], refs[n + 1:]
    copies, virt_copies = start_plane(arrays, rows, gathered, pieces, bufs, virt_buf, sems, 0)
    plane_add(copies, bufs, virt_copies, virt_buf, acc, True)
    out_buf[...] = acc[...].astype(out_buf.dtype)
    pltpu.sync_copy(out_buf, out)


def plane_product(name, arrays, rows, gathered, pieces, dtype):
    n = len(arrays)
    scratch = [pltpu.VMEM((2 * n, *SUM), BF16), pltpu.VMEM((2 * n, *TILE), BF16), pltpu.VMEM(SUM, F32), pltpu.VMEM(SUM, dtype)]
    return call(
        functools.partial(plane_kernel, arrays, rows), name, (gathered, *pieces),
        jax.ShapeDtypeStruct(SUM, dtype), scratch, 4 * n, 2 << 30, 51,
    )


def plane_last_kernel(rows, gathered, top, bottom, sum_in, out, bufs, virt_buf, acc, out_buf, sems):
    sum_copy, = start_all([sum_in], [acc], sems)
    copies, virt_copies = start_plane((6, 7), rows, gathered, (top, bottom), bufs, virt_buf, sems, 1)
    sum_copy.wait()
    plane_add(copies, bufs, virt_copies, virt_buf, acc, False)
    out_buf[...] = acc[...].astype(BF16)
    pltpu.sync_copy(out_buf, out)


def plane_last(rows, gathered, pieces, sum_in):
    scratch = [pltpu.VMEM((4, *SUM), BF16), pltpu.VMEM((4, *TILE), BF16), pltpu.VMEM(SUM, F32), pltpu.VMEM(SUM, BF16)]
    return call(
        functools.partial(plane_last_kernel, rows), "plane_last", (gathered, *pieces, sum_in),
        jax.ShapeDtypeStruct(SUM, BF16), scratch, 9, 1 << 29, 60,
    )


LARGE, DOWN, UP = 2.0**100, 2.0**-24, 2.0**24


def ring_sum(piece_buf, occ_buf, acc, ready):
    for z in range(8):
        ready(z)
        for p in range(PAIR):
            part = jnp.dot(occ_buf[2 * z], piece_buf[z, p, pl.ds(0, HALF), :], preferred_element_type=F32)
            part += jnp.dot(occ_buf[2 * z + 1], piece_buf[z, p, pl.ds(HALF, HALF), :], preferred_element_type=F32)
            at = pl.ds(p * ROWS, ROWS)
            acc[at, :] = part if z == 0 else acc[at, :] + part


def ring_kernel(stride, gap, first, own, other, gathered, *refs):
    out, refs = refs[0], refs[1:]
    if first:
        scale, refs = refs[0], refs[1:]
    piece_buf, occ_buf, acc, out_buf, scale_buf, sems = refs
    core = lax.axis_index("layer")
    own_rows = pl.ds(pl.multiple_of(core * HALF, HALF), HALF)
    other_rows = pl.ds(pl.multiple_of((1 - core) * HALF, HALF), HALF)
    copies = []
    for z in range(8):
        group = []
        for i in range(2):
            tile = pl.ds((2 * z + i) * HALF, HALF)
            k = 2 * z + i
            group += start_all(
                [own.at[tile], other.at[tile]], [occ_buf.at[k, own_rows], occ_buf.at[k, other_rows]], sems, 6 * z + 2 * i
            )
        block = (2 * z + core if first else z) * stride
        for p in range(PAIR):
            start = pl.multiple_of(block + p * (ROWS + gap), HALF)
            group += start_all([gathered.at[pl.ds(start, ROWS)]], [piece_buf.at[z, p]], sems, 6 * z + 4 + p)
        copies.append(group)
    largest = [jnp.zeros((16, COLS), BF16)]

    def ready(z):
        for copy in copies[z]:
            copy.wait()
        if first:
            for k in (2 * z, 2 * z + 1):
                sizes = jnp.abs(occ_buf[k]).reshape(ROWS // 16, 16, COLS)
                largest[0] = jnp.maximum(largest[0], jnp.max(sizes, axis=0))

    ring_sum(piece_buf, occ_buf, acc, ready)
    if first:
        large = jnp.max(largest[0].astype(F32)) > LARGE
        scale_buf[...] = jnp.where(large, UP, 1.0) * jnp.ones_like(scale_buf)

        @pl.when(large)
        def _():
            for k in range(16):
                occ_buf[k] = (occ_buf[k].astype(F32) * DOWN).astype(BF16)
            ring_sum(piece_buf, occ_buf, acc, lambda z: None)

        scale_copy, = start_all([scale_buf], [scale], sems)
    out_buf[...] = acc[...].astype(BF16)
    pltpu.sync_copy(out_buf, out)
    if first:
        scale_copy.wait()


def ring_product(name, own, other, gathered, stride, gap, first):
    scratch = [
        pltpu.VMEM((8, PAIR, ROWS, COLS), BF16), pltpu.VMEM((16, ROWS, COLS), BF16),
        pltpu.VMEM(SUM, F32), pltpu.VMEM(SUM, BF16), pltpu.VMEM((8, BLK), F32),
    ]
    outs = jax.ShapeDtypeStruct(SUM, BF16)
    if first:
        outs = (outs, jax.ShapeDtypeStruct((8, BLK), F32))
    return call(
        functools.partial(ring_kernel, stride, gap, first), name, (own, other, gathered), outs, scratch, 48, 2 << 30, 60
    )


CHUNK = 32


def chi_tile(polar, aux):
    count = aux.shape[0]

    def add_rows(i, total):
        at = pl.ds(pl.multiple_of(i * CHUNK, CHUNK), CHUNK)
        left = [polar[pl.ds(pl.multiple_of(p * ROWS + i * CHUNK, CHUNK), CHUNK), :] for p in range(AUX)]
        left = jnp.concatenate(left, axis=0)
        right = jnp.concatenate([aux[q, at, :] for q in range(count)], axis=0)
        return total + lax.dot_general(left, right, (((1,), (1,)), ((), ())), preferred_element_type=F32)

    shape = (AUX * CHUNK, count * CHUNK)
    total = lax.fori_loop(0, ROWS // CHUNK, add_rows, jnp.zeros(shape, F32), unroll=4)
    rows = lax.broadcasted_iota(jnp.int32, shape, 0)
    cols = lax.broadcasted_iota(jnp.int32, shape, 1)
    total = jnp.where(lax.rem(rows, CHUNK) == lax.rem(cols, CHUNK), total, 0.0)
    sums = [jnp.sum(total[p * CHUNK:(p + 1) * CHUNK], axis=0, keepdims=True) for p in range(AUX)]
    sums = jnp.concatenate(sums + [jnp.zeros((8 - AUX, shape[1]), F32)], axis=0)
    group = lax.broadcasted_iota(jnp.int32, sums.shape, 1) // CHUNK
    rows = lax.broadcasted_iota(jnp.int32, (8, BLK), 0)
    cols = lax.broadcasted_iota(jnp.int32, (8, BLK), 1)
    result = jnp.zeros((8, BLK), F32)
    for q in range(count):
        value = jnp.sum(jnp.where(group == q, sums, 0.0), axis=1, keepdims=True)
        result = jnp.where(cols == rows * count + q, value, result)
    return jnp.sum(result, axis=0, keepdims=True)


def polar_kernel(gathered, top, bottom, plane_sum, ring_part, own_aux, other_aux, scale, polar, chi,
                 bufs, virt_buf, acc, aux_buf, polar_buf, chi_buf, scale_buf, sems):
    core = lax.axis_index("layer")
    own, other = pl.ds(core * AUX, AUX), pl.ds((1 - core) * AUX, AUX)
    sum_copy, = start_all((plane_sum,), (acc,), sems)
    copies, virt_copies = start_plane((6, 7), PAIR * ROWS, gathered, (top, bottom), bufs, virt_buf, sems, 4)
    part_copies = start_all(
        (ring_part, own_aux, other_aux),
        (polar_buf.at[pl.ds(0, PAIR * ROWS)], aux_buf.at[own], aux_buf.at[other]), sems, 1
    )
    scale_copy, = start_all((scale,), (scale_buf,), sems, 12)
    sum_copy.wait()
    plane_add(copies, bufs, virt_copies, virt_buf, acc, False)
    scale_copy.wait()
    factor = jnp.broadcast_to(scale_buf[pl.ds(0, 1), pl.ds(0, 1)], SUM)
    polar_buf[pl.ds(PAIR * ROWS, PAIR * ROWS), :] = (acc[...] * factor).astype(BF16)
    for copy in part_copies:
        copy.wait()
    polar_copy, = start_all((polar_buf,), (polar,), sems)
    chi_buf[...] = jnp.broadcast_to(chi_tile(polar_buf, aux_buf), chi_buf.shape)
    pltpu.sync_copy(chi_buf, chi)
    polar_copy.wait()


def polar_product(gathered, pieces, plane_sum, ring_part, own_aux, other_aux, scale):
    outs = (jax.ShapeDtypeStruct((AUX * ROWS, COLS), BF16), jax.ShapeDtypeStruct((128, BLK), F32))
    scratch = [pltpu.VMEM((4, *SUM), BF16), pltpu.VMEM((4, *TILE), BF16), pltpu.VMEM(SUM, F32)]
    scratch += [pltpu.VMEM((2 * AUX, ROWS, COLS), BF16)] + buffers_of((*outs, scale))
    operands = (gathered, *pieces, plane_sum, ring_part, own_aux, other_aux, scale)
    return call(polar_kernel, "polar_product", operands, outs, scratch, 13, 1 << 29, 60)


def body(integrals, density_occ, density_virt, mask_int, mask_occ, mask_virt):
    plane_aux, ring_aux, own_aux = mask_inputs(
        mask_int, mask_occ, mask_virt, integrals, density_occ, density_virt
    )
    gathered = lax.all_gather(ring_aux, ("row", "layer"), axis=0, tiled=True)
    plane = gather_plane(plane_aux)
    plane_sum = plane_product("plane_near", tuple(range(6)), STRIDE, gathered, plane[:6], F32)
    *far, plane_sum = lax.optimization_barrier((*plane[6:], plane_sum))
    own_occ = occ_tiles((*plane[:6], *far))
    other_occ = swap_cores(own_occ)
    half_tensor = plane_last(STRIDE, gathered, far, plane_sum)
    own_occ, other_occ, half_tensor = lax.optimization_barrier((own_occ, other_occ, half_tensor))
    occ_first, scale = ring_product("occ_first", own_occ, other_occ, gathered, STRIDE, HALF, True)

    ring = lax.all_gather(half_tensor, "row", axis=0, tiled=True)
    own_aux, occ_first = lax.optimization_barrier((own_aux, occ_first))
    other_aux = swap_cores(own_aux)
    plane = gather_plane(occ_first)
    plane_sum = plane_product("plane_near", tuple(range(6)), PAIR * ROWS, gathered, plane[:6], F32)
    ring_part = ring_product("polar_ring", own_occ, other_occ, ring, PAIR * ROWS, 0, False)
    polar, chi = polar_product(gathered, plane[6:], plane_sum, ring_part, own_aux, other_aux, scale)

    shares = lax.all_to_all(chi.reshape(128, 1, BLK), ("row", "col"), 0, 0)
    chi = jnp.sum(shares.reshape(128, BLK), axis=0) * (1.0 / (ROWS * lax.axis_size("row")))
    return polar.reshape(AUX, ROWS, COLS), chi[:2 * AUX * AUX].reshape(AUX, 2 * AUX)


def solution(mesh):
    in_specs = (
        P("layer", "row", "col"),
        P("row", "col"),
        P("row", "col"),
        P("layer", "row", "col"),
        P("row", "col"),
        P("row", "col"),
    )
    out_specs = (P("layer", "row", "col"), P("layer", None))
    return jax.shard_map(body, mesh=mesh, in_specs=in_specs, out_specs=out_specs, check_vma=False)
```

```python
import functools

import jax
import jax.numpy as jnp
from jax import lax
from jax.experimental import pallas as pl
from jax.experimental.pallas import tpu as pltpu
from jax.sharding import PartitionSpec as P

BLK = 128
ROWS = 512
COLS = 256
HALF = 256
PAIR = 2
AUX = 2 * PAIR
STRIDE = PAIR * ROWS + HALF
F32 = jnp.float32
BF16 = jnp.bfloat16
HBM = pl.BlockSpec(memory_space=pltpu.HBM)
ANY = pl.BlockSpec(memory_space=pl.ANY)
PARAMS = pltpu.CompilerParams(vmem_limit_bytes=60 * 1024 * 1024)


def plane_index(y, x, core):
    return ((y % 4) * 4 + x % 4) * 2 + core


def plane_perm(shift, first):
    pairs = []
    for y in range(4):
        for x in range(4):
            for core in range(2):
                along_x = (core == 0) == first
                to = (y, x + shift) if along_x else (y + shift, x)
                pairs.append((plane_index(y, x, core), plane_index(*to, core)))
    return pairs


def plane_move(value, shift, first):
    return lax.ppermute(value, ("col", "layer"), plane_perm(shift, first))


def swap_cores(value):
    return lax.ppermute(value, "layer", [(0, 1), (1, 0)])


PLANE = (
    ((0, 0), (-1, 0)),
    ((1, 0), (2, 0)),
    ((0, -1), (-1, -1)),
    ((0, 1), (-1, 1)),
    ((1, -1), (2, -1)),
    ((1, 1), (2, 1)),
    ((0, 2), (-1, 2)),
    ((1, 2), (2, 2)),
)


def gather_plane(plane):
    rows = plane.shape[0]
    half = rows // 2
    before, behind = plane_move(plane, 1, True), plane_move(plane, -1, True)
    low, high = plane_move(before[:half], 1, True), plane_move(behind[half:], -1, True)
    top, = pack((plane, before), ((0, 0, rows, 0, 0), (1, 0, rows, 0, rows)), (2 * rows,))
    top_before, top_behind = plane_move(top, 1, False), plane_move(top, -1, False)
    bottom, = pack(
        (behind, low, high),
        ((0, 0, rows, 0, 0), (1, 0, half, 0, rows), (2, 0, half, 0, rows + half)),
        (2 * rows,),
    )
    bottom_before, bottom_behind = plane_move(bottom, 1, False), plane_move(bottom, -1, False)
    top_before, top_behind, bottom_before, bottom_behind = lax.optimization_barrier(
        (top_before, top_behind, bottom_before, bottom_behind)
    )
    top_far, bottom_far = plane_move(top_before, 1, False), plane_move(bottom_behind, -1, False)
    return top, bottom, top_before, top_behind, bottom_before, bottom_behind, top_far, bottom_far


def buffers_of(arrays):
    return [pltpu.VMEM(a.shape, a.dtype) for a in arrays]


def start_all(sources, buffers, sems, first=0):
    copies = [pltpu.make_async_copy(a, b, sems.at[first + i]) for i, (a, b) in enumerate(zip(sources, buffers))]
    for copy in copies:
        copy.start()
    return copies


def pack_kernel(moves, count, *refs):
    sources, outs, buf, sems = refs[:count], refs[count:-2], refs[-2], refs[-1]
    loads, stores, at = [], [], 0
    for k, (i, start, rows, o, to) in enumerate(moves):
        part = buf.at[pl.ds(at, rows)]
        loads.append(pltpu.make_async_copy(sources[i].at[pl.ds(start, rows)], part, sems.at[0, k]))
        stores.append(pltpu.make_async_copy(part, outs[o].at[pl.ds(to, rows)], sems.at[1, k]))
        at += rows
    for load in loads:
        load.start()
    for load, store in zip(loads, stores):
        load.wait()
        store.start()
    for store in stores:
        store.wait()


def pack(sources, moves, out_rows):
    return pl.pallas_call(
        functools.partial(pack_kernel, moves, len(sources)),
        out_shape=tuple(jax.ShapeDtypeStruct((rows, COLS), BF16) for rows in out_rows),
        in_specs=[ANY] * len(sources),
        out_specs=(HBM,) * len(out_rows),
        scratch_shapes=[
            pltpu.VMEM((sum(move[2] for move in moves), COLS), BF16),
            pltpu.SemaphoreType.DMA((2, len(moves))),
        ],
        compiler_params=pltpu.CompilerParams(vmem_limit_bytes=8 * 1024 * 1024),
        cost_estimate=pl.CostEstimate(flops=0, bytes_accessed=4 << 20, transcendentals=0),
        name="pack",
    )(*sources)


def mask_kernel(mask_int, mask_occ, mask_virt, integrals, occ, virt, plane, ring, aux,
                int_buf, occ_buf, virt_buf, int_weight, occ_weight, virt_weight, load, store):
    core = lax.axis_index("layer")
    half = pl.ds(pl.multiple_of(core * HALF, HALF), HALF)
    weights = start_all((mask_int, mask_occ, mask_virt), (int_weight, occ_weight, virt_weight), load)
    loads = start_all([integrals.at[p] for p in range(AUX)], [int_buf.at[p] for p in range(AUX)], load, 3)
    loads += start_all([virt.at[half], occ.at[half]], [virt_buf, occ_buf], load, 3 + AUX)

    def mask(ref, weight, block_rows):
        for i in range(block_rows):
            for j in range(COLS // BLK):
                at = pl.ds(i * BLK, BLK), pl.ds(j * BLK, BLK)
                block = ref[at].astype(F32)
                ref[at] = (block * jnp.broadcast_to(weight(i, j).astype(F32), block.shape)).astype(BF16)

    def half_weight(ref):
        def weight(i, j):
            low, high = ref[pl.ds(j, 1), pl.ds(i, 1)], ref[pl.ds(j, 1), pl.ds(HALF // BLK + i, 1)]
            return jnp.where(core == 0, low, high)

        return weight

    for copy in weights:
        copy.wait()
    stores = []
    for p in range(AUX):
        loads[p].wait()
        mask(int_buf.at[p], lambda i, j: int_weight[p, pl.ds(j, 1), pl.ds(i, 1)], ROWS // BLK)
        if p < PAIR:
            to = plane.at[pl.ds(p * ROWS, ROWS)]
        else:
            to = ring.at[pl.ds((p - PAIR) * (ROWS + HALF), ROWS)]
        stores += start_all([int_buf.at[p], int_buf.at[p]], [to, aux.at[p]], store, 2 * p)
    loads[AUX].wait()
    mask(virt_buf, half_weight(virt_weight), HALF // BLK)
    stores += start_all([virt_buf], [ring.at[pl.ds(ROWS, HALF)]], store, 2 * AUX)
    loads[AUX + 1].wait()
    mask(occ_buf, half_weight(occ_weight), HALF // BLK)
    stores += start_all([occ_buf], [plane.at[pl.ds(PAIR * ROWS, HALF)]], store, 2 * AUX + 1)
    for copy in stores:
        copy.wait()


def mask_inputs(mask_int, mask_occ, mask_virt, integrals, occ, virt):
    outs = (
        jax.ShapeDtypeStruct((STRIDE, COLS), BF16),
        jax.ShapeDtypeStruct((STRIDE, COLS), BF16),
        jax.ShapeDtypeStruct((AUX, ROWS, COLS), BF16),
    )
    masks = (mask_int.transpose(0, 2, 1), mask_occ.T, mask_virt.T)
    return pl.pallas_call(
        mask_kernel,
        out_shape=outs,
        in_specs=[HBM] * 6,
        out_specs=(HBM,) * 3,
        scratch_shapes=[pltpu.VMEM((AUX, ROWS, COLS), BF16)]
        + [pltpu.VMEM((HALF, COLS), BF16)] * 2
        + [pltpu.VMEM(a.shape, a.dtype) for a in masks]
        + [pltpu.SemaphoreType.DMA((5 + AUX,)), pltpu.SemaphoreType.DMA((2 + 2 * AUX,))],
        compiler_params=PARAMS,
        name="mask_inputs",
    )(*masks, integrals, occ, virt)


def tile_index(offsets):
    col, core = lax.axis_index("col"), lax.axis_index("layer")
    y, x = lax.div(col, 4), lax.rem(col, 4)
    first, second = offsets
    tile_x = lax.rem(x + jnp.where(core == 0, first, second) + 4, 4)
    tile_y = lax.rem(y + jnp.where(core == 0, second, first) + 4, 4)
    return tile_y * 4 + tile_x


def call(kernel, name, operands, outs, scratch, sems, flops, vmem):
    return pl.pallas_call(
        kernel,
        out_shape=outs,
        in_specs=[HBM] * len(operands),
        out_specs=jax.tree.map(lambda _: HBM, outs),
        scratch_shapes=scratch + [pltpu.SemaphoreType.DMA((sems,))],
        compiler_params=pltpu.CompilerParams(vmem_limit_bytes=vmem * 1024 * 1024),
        cost_estimate=pl.CostEstimate(flops=flops, bytes_accessed=9 << 20, transcendentals=0),
        name=name,
    )(*operands)


SUM = (PAIR * ROWS, COLS)
TILE = (HALF, COLS)


def occ_kernel(*refs):
    n = len(PLANE)
    pieces, out, buf, sems = refs[:n], refs[n], refs[n + 1], refs[n + 2]
    loads, stores = [], []
    for a, tiles in enumerate(PLANE):
        for k, offsets in enumerate(tiles):
            i = 2 * a + k
            source = pieces[a].at[pl.ds(k * STRIDE + PAIR * ROWS, HALF)]
            to = out.at[pl.ds(pl.multiple_of(tile_index(offsets) * HALF, HALF), HALF)]
            loads.append(pltpu.make_async_copy(source, buf.at[i], sems.at[i]))
            stores.append(pltpu.make_async_copy(buf.at[i], to, sems.at[2 * n + i]))
    for load in loads:
        load.start()
    for load, store in zip(loads, stores):
        load.wait()
        store.start()
    for store in stores:
        store.wait()


def occ_tiles(pieces):
    return call(
        occ_kernel, "occ_tiles", pieces, jax.ShapeDtypeStruct((16 * HALF, COLS), BF16),
        [pltpu.VMEM((16, *TILE), BF16)], 32, 0, 60,
    )


def start_plane(arrays, rows, gathered, pieces, bufs, virt_buf, sems, first):
    copies, virt_copies = [], []
    for k, a in enumerate(arrays):
        for i, offsets in enumerate(PLANE[a]):
            sem = first + 4 * k + 2 * i
            source = pieces[k].at[pl.ds(i * rows, PAIR * ROWS)]
            copies += start_all([source], [bufs.at[2 * k + i]], sems, sem)
            start = pl.multiple_of(tile_index(offsets) * STRIDE + ROWS, HALF)
            virt_copies += start_all([gathered.at[pl.ds(start, HALF)]], [virt_buf.at[2 * k + i]], sems, sem + 1)
    return copies, virt_copies


def plane_add(copies, bufs, virt_copies, virt, acc, fresh):
    for k in range(0, len(copies), 2):
        for copy in copies[k:k + 2] + virt_copies[k:k + 2]:
            copy.wait()
        for p in range(PAIR):
            at = pl.ds(p * ROWS, ROWS)
            part = jnp.dot(bufs[k, at, :], virt[k], preferred_element_type=F32)
            part += jnp.dot(bufs[k + 1, at, :], virt[k + 1], preferred_element_type=F32)
            acc[at, :] = part if fresh and k == 0 else acc[at, :] + part


def plane_kernel(arrays, rows, gathered, *refs):
    n = len(arrays)
    pieces, out, (bufs, virt_buf, acc, out_buf, sems) = refs[:n], refs[n], refs[n + 1:]
    copies, virt_copies = start_plane(arrays, rows, gathered, pieces, bufs, virt_buf, sems, 0)
    plane_add(copies, bufs, virt_copies, virt_buf, acc, True)
    out_buf[...] = acc[...].astype(out_buf.dtype)
    pltpu.sync_copy(out_buf, out)


def plane_product(name, arrays, rows, gathered, pieces, dtype):
    n = len(arrays)
    scratch = [pltpu.VMEM((2 * n, *SUM), BF16), pltpu.VMEM((2 * n, *TILE), BF16), pltpu.VMEM(SUM, F32), pltpu.VMEM(SUM, dtype)]
    return call(
        functools.partial(plane_kernel, arrays, rows), name, (gathered, *pieces),
        jax.ShapeDtypeStruct(SUM, dtype), scratch, 4 * n, 2 << 30, 51,
    )


def plane_last_kernel(rows, gathered, top, bottom, sum_in, out, bufs, virt_buf, acc, out_buf, sems):
    sum_copy, = start_all([sum_in], [acc], sems)
    copies, virt_copies = start_plane((6, 7), rows, gathered, (top, bottom), bufs, virt_buf, sems, 1)
    sum_copy.wait()
    plane_add(copies, bufs, virt_copies, virt_buf, acc, False)
    out_buf[...] = acc[...].astype(BF16)
    pltpu.sync_copy(out_buf, out)


def plane_last(rows, gathered, pieces, sum_in):
    scratch = [pltpu.VMEM((4, *SUM), BF16), pltpu.VMEM((4, *TILE), BF16), pltpu.VMEM(SUM, F32), pltpu.VMEM(SUM, BF16)]
    return call(
        functools.partial(plane_last_kernel, rows), "plane_last", (gathered, *pieces, sum_in),
        jax.ShapeDtypeStruct(SUM, BF16), scratch, 9, 1 << 29, 60,
    )


LARGE, DOWN, UP = 2.0**100, 2.0**-24, 2.0**24


def ring_sum(piece_buf, occ_buf, acc, ready):
    for z in range(8):
        ready(z)
        for p in range(PAIR):
            part = jnp.dot(occ_buf[2 * z], piece_buf[z, p, pl.ds(0, HALF), :], preferred_element_type=F32)
            part += jnp.dot(occ_buf[2 * z + 1], piece_buf[z, p, pl.ds(HALF, HALF), :], preferred_element_type=F32)
            at = pl.ds(p * ROWS, ROWS)
            acc[at, :] = part if z == 0 else acc[at, :] + part


def ring_kernel(stride, gap, first, own, other, gathered, *refs):
    out, refs = refs[0], refs[1:]
    if first:
        scale, refs = refs[0], refs[1:]
    piece_buf, occ_buf, acc, out_buf, scale_buf, sems = refs
    core = lax.axis_index("layer")
    own_rows = pl.ds(pl.multiple_of(core * HALF, HALF), HALF)
    other_rows = pl.ds(pl.multiple_of((1 - core) * HALF, HALF), HALF)
    copies = []
    for z in range(8):
        group = []
        for i in range(2):
            tile = pl.ds((2 * z + i) * HALF, HALF)
            k = 2 * z + i
            group += start_all(
                [own.at[tile], other.at[tile]], [occ_buf.at[k, own_rows], occ_buf.at[k, other_rows]], sems, 6 * z + 2 * i
            )
        block = (2 * z + core if first else z) * stride
        for p in range(PAIR):
            start = pl.multiple_of(block + p * (ROWS + gap), HALF)
            group += start_all([gathered.at[pl.ds(start, ROWS)]], [piece_buf.at[z, p]], sems, 6 * z + 4 + p)
        copies.append(group)
    largest = [jnp.zeros((16, COLS), BF16)]

    def ready(z):
        for copy in copies[z]:
            copy.wait()
        if first:
            for k in (2 * z, 2 * z + 1):
                sizes = jnp.abs(occ_buf[k]).reshape(ROWS // 16, 16, COLS)
                largest[0] = jnp.maximum(largest[0], jnp.max(sizes, axis=0))

    ring_sum(piece_buf, occ_buf, acc, ready)
    if first:
        large = jnp.max(largest[0].astype(F32)) > LARGE
        scale_buf[...] = jnp.where(large, UP, 1.0) * jnp.ones_like(scale_buf)

        @pl.when(large)
        def _():
            for k in range(16):
                occ_buf[k] = (occ_buf[k].astype(F32) * DOWN).astype(BF16)
            ring_sum(piece_buf, occ_buf, acc, lambda z: None)

        scale_copy, = start_all([scale_buf], [scale], sems)
    out_buf[...] = acc[...].astype(BF16)
    pltpu.sync_copy(out_buf, out)
    if first:
        scale_copy.wait()


def ring_product(name, own, other, gathered, stride, gap, first):
    scratch = [
        pltpu.VMEM((8, PAIR, ROWS, COLS), BF16), pltpu.VMEM((16, ROWS, COLS), BF16),
        pltpu.VMEM(SUM, F32), pltpu.VMEM(SUM, BF16), pltpu.VMEM((8, BLK), F32),
    ]
    outs = jax.ShapeDtypeStruct(SUM, BF16)
    if first:
        outs = (outs, jax.ShapeDtypeStruct((8, BLK), F32))
    return call(
        functools.partial(ring_kernel, stride, gap, first), name, (own, other, gathered), outs, scratch, 48, 2 << 30, 51 if first else 60
    )


CHUNK = 32


def chi_tile(polar, aux):
    count = aux.shape[0]

    def add_rows(i, total):
        at = pl.ds(pl.multiple_of(i * CHUNK, CHUNK), CHUNK)
        left = [polar[pl.ds(pl.multiple_of(p * ROWS + i * CHUNK, CHUNK), CHUNK), :] for p in range(AUX)]
        left = jnp.concatenate(left, axis=0)
        right = jnp.concatenate([aux[q, at, :] for q in range(count)], axis=0)
        return total + lax.dot_general(left, right, (((1,), (1,)), ((), ())), preferred_element_type=F32)

    shape = (AUX * CHUNK, count * CHUNK)
    total = lax.fori_loop(0, ROWS // CHUNK, add_rows, jnp.zeros(shape, F32), unroll=4)
    rows = lax.broadcasted_iota(jnp.int32, shape, 0)
    cols = lax.broadcasted_iota(jnp.int32, shape, 1)
    total = jnp.where(lax.rem(rows, CHUNK) == lax.rem(cols, CHUNK), total, 0.0)
    sums = [jnp.sum(total[p * CHUNK:(p + 1) * CHUNK], axis=0, keepdims=True) for p in range(AUX)]
    sums = jnp.concatenate(sums + [jnp.zeros((8 - AUX, shape[1]), F32)], axis=0)
    group = lax.broadcasted_iota(jnp.int32, sums.shape, 1) // CHUNK
    rows = lax.broadcasted_iota(jnp.int32, (8, BLK), 0)
    cols = lax.broadcasted_iota(jnp.int32, (8, BLK), 1)
    result = jnp.zeros((8, BLK), F32)
    for q in range(count):
        value = jnp.sum(jnp.where(group == q, sums, 0.0), axis=1, keepdims=True)
        result = jnp.where(cols == rows * count + q, value, result)
    return jnp.sum(result, axis=0, keepdims=True)


def polar_kernel(gathered, top, bottom, plane_sum, ring_part, own_aux, other_aux, scale, polar, chi,
                 bufs, virt_buf, acc, aux_buf, polar_buf, chi_buf, scale_buf, sems):
    core = lax.axis_index("layer")
    own, other = pl.ds(core * AUX, AUX), pl.ds((1 - core) * AUX, AUX)
    sum_copy, = start_all((plane_sum,), (acc,), sems)
    copies, virt_copies = start_plane((6, 7), PAIR * ROWS, gathered, (top, bottom), bufs, virt_buf, sems, 4)
    part_copies = start_all(
        (ring_part, own_aux, other_aux),
        (polar_buf.at[pl.ds(0, PAIR * ROWS)], aux_buf.at[own], aux_buf.at[other]), sems, 1
    )
    scale_copy, = start_all((scale,), (scale_buf,), sems, 12)
    sum_copy.wait()
    plane_add(copies, bufs, virt_copies, virt_buf, acc, False)
    scale_copy.wait()
    factor = jnp.broadcast_to(scale_buf[pl.ds(0, 1), pl.ds(0, 1)], SUM)
    polar_buf[pl.ds(PAIR * ROWS, PAIR * ROWS), :] = (acc[...] * factor).astype(BF16)
    for copy in part_copies:
        copy.wait()
    polar_copy, = start_all((polar_buf,), (polar,), sems)
    chi_buf[...] = jnp.broadcast_to(chi_tile(polar_buf, aux_buf), chi_buf.shape)
    pltpu.sync_copy(chi_buf, chi)
    polar_copy.wait()


def polar_product(gathered, pieces, plane_sum, ring_part, own_aux, other_aux, scale):
    outs = (jax.ShapeDtypeStruct((AUX * ROWS, COLS), BF16), jax.ShapeDtypeStruct((128, BLK), F32))
    scratch = [pltpu.VMEM((4, *SUM), BF16), pltpu.VMEM((4, *TILE), BF16), pltpu.VMEM(SUM, F32)]
    scratch += [pltpu.VMEM((2 * AUX, ROWS, COLS), BF16)] + buffers_of((*outs, scale))
    operands = (gathered, *pieces, plane_sum, ring_part, own_aux, other_aux, scale)
    return call(polar_kernel, "polar_product", operands, outs, scratch, 13, 1 << 29, 60)


def body(integrals, density_occ, density_virt, mask_int, mask_occ, mask_virt):
    plane_aux, ring_aux, own_aux = mask_inputs(
        mask_int, mask_occ, mask_virt, integrals, density_occ, density_virt
    )
    gathered = lax.all_gather(ring_aux, ("row", "layer"), axis=0, tiled=True)
    plane = gather_plane(plane_aux)
    plane_sum = plane_product("plane_near", tuple(range(6)), STRIDE, gathered, plane[:6], F32)
    *far, plane_sum = lax.optimization_barrier((*plane[6:], plane_sum))
    own_occ = occ_tiles((*plane[:6], *far))
    other_occ = swap_cores(own_occ)
    half_tensor = plane_last(STRIDE, gathered, far, plane_sum)
    own_occ, other_occ, half_tensor = lax.optimization_barrier((own_occ, other_occ, half_tensor))
    occ_first, scale = ring_product("occ_first", own_occ, other_occ, gathered, STRIDE, HALF, True)

    ring = lax.all_gather(half_tensor, "row", axis=0, tiled=True)
    own_aux, occ_first = lax.optimization_barrier((own_aux, occ_first))
    other_aux = swap_cores(own_aux)
    plane = gather_plane(occ_first)
    plane_sum = plane_product("plane_near", tuple(range(6)), PAIR * ROWS, gathered, plane[:6], F32)
    ring_part = ring_product("polar_ring", own_occ, other_occ, ring, PAIR * ROWS, 0, False)
    polar, chi = polar_product(gathered, plane[6:], plane_sum, ring_part, own_aux, other_aux, scale)

    shares = lax.all_to_all(chi.reshape(128, 1, BLK), ("row", "col"), 0, 0)
    chi = jnp.sum(shares.reshape(128, BLK), axis=0) * (1.0 / (ROWS * lax.axis_size("row")))
    return polar.reshape(AUX, ROWS, COLS), chi[:2 * AUX * AUX].reshape(AUX, 2 * AUX)


def solution(mesh):
    in_specs = (
        P("layer", "row", "col"),
        P("row", "col"),
        P("row", "col"),
        P("layer", "row", "col"),
        P("row", "col"),
        P("row", "col"),
    )
    out_specs = (P("layer", "row", "col"), P("layer", None))
    return jax.shard_map(body, mesh=mesh, in_specs=in_specs, out_specs=out_specs, check_vma=False)
```
